128 devices in a mesh: row: 32 (over y, z_hi, x), frame: 2 (over core), coil: 2 (over z_lo).
Axes of the slice: x: 4, y: 4, z: 4 (z_hi: 2, z_lo: 2; z = z_hi * 2 + z_lo), core: 2. Of those that a mesh axis runs over, the one named last changes fastest.
Arguments:
- factor_u: bfloat16 [2, 48, 1024, 1024], P(None, None, 'row'), may hold values from -4 to 4
- temporal_v: bfloat16 [2, 48], replicated, may hold values from -4 to 4
- sensitivity: bfloat16 [2, 16, 1024, 1024], P(None, 'coil', 'row'), may hold values from -4 to 4
- kspace_data: bfloat16 [2, 2, 16, 1024, 1024], P(None, 'frame', 'coil', 'row'), may hold values from -6 to 6
- sample_mask: int32 [2, 1024], P('frame'), may hold values 0 or 1
- tv_weight: float32 [1024, 1024], P('row'), may hold values from 0.5 to 2
Outputs:
- factor_grad: float32 [2, 48, 1024, 1024], P(None, None, 'row')
The draws below stay inside these ranges and needn't reach their ends.
Inputs may be any that keep to these rules, and one draw needn't show every extreme that they name: `sample_mask`: 1 marks a sampled line.
All inputs are finite; a program needn't handle non-finite values. No bound on the sum of `sample_mask` on one device may be relied on, other than what follows from the above.
Results may differ from the reference program's by a relative error of at most 0.007.
Values may be sent and summed in bfloat16 or wider, within the bound.
A program may use at most 192 MiB of HBM per device.

```python
import math
import jax
import jax.numpy as jnp
from jax import lax

N = 1024
C = 16
R = 48
T_SIZE = 2


def plant(values, stream_key, least, high):
    longest = values.shape.index(max(values.shape))
    spots = []
    for shift in (0, 1):
        where = [jax.random.randint(jax.random.fold_in(stream_key, axis), (), 0, length) for axis, length in enumerate(values.shape)]
        where[longest] = (where[longest] + shift) % values.shape[longest]
        spots.append(tuple(where))
    return values.at[spots[0]].set(least).at[spots[1]].set(high)


def block_levels(key, extent, shards, smallest, high):
    gain = 1.0
    for axis_at, blocks in shards:
        steps = jax.random.uniform(jax.random.fold_in(jax.random.fold_in(key, 6), axis_at), (blocks,), jnp.float32, smallest / len(shards), high / len(shards))
        gain = gain * jnp.repeat(jnp.exp(steps), extent[axis_at] // blocks).reshape((-1,) + (1,) * (len(extent) - 1 - axis_at))
    return gain


def normal_values(own_key, shape, scale, limit, shards=(), held_as=jnp.bfloat16):
    drawn = scale * jax.random.normal(own_key, shape, jnp.float32)
    if shards:
        drawn = drawn * block_levels(own_key, shape, shards, -0.22, 0.18)
    return jnp.clip(drawn, -limit, limit).astype(held_as)


def setup_inputs(seed: int = 0) -> dict:
    key_of = jax.random.split(jax.random.key(seed), 7)
    return {
        "factor_u": normal_values(key_of[0], (2, R, N, N), 0.3, 4.0, ((2, 32),)),
        "temporal_v": normal_values(key_of[1], (T_SIZE, R), T_SIZE ** -0.5, 4.0),
        "sensitivity": normal_values(key_of[2], (2, C, N, N), 0.25, 4.0, ((1, 2), (2, 32))),
        "kspace_data": normal_values(key_of[3], (2, T_SIZE, C, N, N), 1.0, 6.0, ((1, 2), (2, 2), (3, 32))),
        "sample_mask": plant((jax.random.randint(key_of[4], (T_SIZE, N), 0, 3) < 1).astype(jnp.int32), jax.random.fold_in(key_of[4], 1), 0, 1),
        "tv_weight": jnp.clip(jnp.exp(math.log(2.0) - 1.3862944 * jax.random.uniform(key_of[5], (N, N), jnp.float32) ** block_levels(key_of[5], (N, N), ((0, 32),), -0.2, 0.2)), 0.5, 2.0),
    }


tv_eps = 0.25
tv_gain = 0.5

def rounded(values):
    return lax.optimization_barrier(values.astype(jnp.bfloat16)).astype(jnp.float32)

def tv_gradient(frame_image, weights):
    zero_col = jnp.zeros_like(frame_image[..., :1])
    zero_row = jnp.zeros_like(frame_image[..., :1, :])
    across = jnp.concatenate([frame_image[..., 1:] - frame_image[..., :-1], zero_col], axis=-1)
    down_diff = jnp.concatenate([frame_image[..., 1:, :] - frame_image[..., :-1, :], zero_row], axis=-2)
    magnitude = jnp.sqrt(across[0] * across[0] + across[1] * across[1] + down_diff[0] * down_diff[0] + down_diff[1] * down_diff[1] + tv_eps)
    flux_across = weights * across / magnitude
    flux_down = weights * down_diff / magnitude
    back_across = jnp.concatenate([zero_col, flux_across[..., :-1]], axis=-1) - flux_across
    back_down = jnp.concatenate([zero_row, flux_down[..., :-1, :]], axis=-2) - flux_down
    return back_across + back_down

def reference(factor_u, temporal_v, sensitivity, kspace_data, sample_mask, tv_weight):
    factor = factor_u.astype(jnp.float32)
    temporal = temporal_v.astype(jnp.float32)
    coil_maps = sensitivity.astype(jnp.float32)

    def one_frame(inputs):
        frame_v, frame_data, frame_mask = inputs
        frame_image = jnp.einsum('prij,r->pij', factor, frame_v, precision=lax.Precision.HIGHEST)
        coil_real = rounded(coil_maps[0] * frame_image[0] - coil_maps[1] * frame_image[1])
        coil_imag = rounded(coil_maps[0] * frame_image[1] + coil_maps[1] * frame_image[0])
        coil_image = lax.complex(coil_real, coil_imag)
        half_spectrum = jnp.fft.fft(coil_image, axis=-1, norm='ortho')
        half_spectrum = lax.complex(rounded(jnp.real(half_spectrum)), rounded(jnp.imag(half_spectrum)))
        spectrum = jnp.fft.fft(half_spectrum, axis=-2, norm='ortho')
        measured_data = frame_data.astype(jnp.float32)
        measured = jnp.swapaxes(lax.complex(measured_data[0], measured_data[1]), -1, -2)
        sample_keep = frame_mask.astype(jnp.float32)[None, :, None]
        misfit = spectrum - measured
        misfit = lax.complex(rounded(sample_keep * jnp.real(misfit)), rounded(sample_keep * jnp.imag(misfit)))
        back_half = jnp.fft.ifft(misfit, axis=-2, norm='ortho')
        back_half = lax.complex(rounded(jnp.real(back_half)), rounded(jnp.imag(back_half)))
        back_image = jnp.fft.ifft(back_half, axis=-1, norm='ortho')
        back_real = jnp.real(back_image)
        back_imag = jnp.imag(back_image)
        data_real = lax.optimization_barrier(jnp.sum(coil_maps[0] * back_real + coil_maps[1] * back_imag, axis=0))
        data_imag = lax.optimization_barrier(jnp.sum(coil_maps[0] * back_imag - coil_maps[1] * back_real, axis=0))
        data_grad = jnp.stack([data_real, data_imag])
        return data_grad + tv_gain * tv_gradient(frame_image, tv_weight)
    frame_grad = lax.map(one_frame, (temporal, jnp.moveaxis(kspace_data, 1, 0), sample_mask))
    return jnp.einsum('tpij,tr->prij', frame_grad, temporal, precision=lax.Precision.HIGHEST)
```

```python
import math

import jax
import jax.numpy as jnp
import numpy as np
from jax import lax
from jax.experimental import pallas as pl
from jax.experimental.pallas import tpu as pltpu
from jax.sharding import PartitionSpec as P

N = 1024
ROWS = 32
RANK = 48
COILS = 8
GROUPS = 2
PER = COILS // GROUPS
DEVS = 32
TV_EPS = 0.25
TV_GAIN = 0.5
F32 = jnp.float32
BF16 = jnp.bfloat16


def fourier_tables():
    position = np.arange(N)
    angle = 2.0 * math.pi * ((position[:, None] * position[None, :]) % N) / N
    both = np.stack([np.cos(angle), np.sin(angle)]) / math.sqrt(N)
    return both.astype(jnp.bfloat16)


def swap_blocks(parts):
    lane = lax.broadcasted_iota(jnp.int32, parts[0].shape, 1)
    even = (lane // 32) % 2 == 0
    low = lane < 64
    a = list(parts)
    for x, y in ((0, 1), (2, 3)):
        first = jnp.where(even, a[x], pltpu.roll(a[y], 32, 1))
        second = jnp.where(even, pltpu.roll(a[x], 96, 1), a[y])
        a[x], a[y] = first, second
    for x, y in ((0, 2), (1, 3)):
        first = jnp.where(low, a[x], pltpu.roll(a[y], 64, 1))
        second = jnp.where(low, pltpu.roll(a[x], 64, 1), a[y])
        a[x], a[y] = first, second
    return a


def dot(a, b):
    return jnp.dot(a, b, preferred_element_type=F32)


def main_kernel(
    v_ref, mask_ref, u_hbm, s_hbm, d_hbm, w_hbm, tab_hbm, out_ref,
    u, s, d, w, tab, f, a, dt, mcol, x, land, mis, b, r, lmat, acc, halo_s, halo_r, part_s, part_r, comb, tvg,
    u_sem, in_sem, halo_send, halo_recv, x_send, x_recv, b_send, b_recv, p_send, p_recv, c_send, c_recv,
):
    row = lax.axis_index("row")
    frame = lax.axis_index("frame")
    coil = lax.axis_index("coil")
    my_y = row // 8

    u_copies = []
    for q in range(4):
        part = (q // 2, slice(None), pl.ds((q % 2) * 16, 16))
        u_copies.append(pltpu.make_async_copy(u_hbm.at[part], u.at[part], u_sem.at[q]))
    for copy in u_copies:
        copy.start()
    in_copies = [
        pltpu.make_async_copy(src, dst, in_sem.at[q])
        for q, (src, dst) in enumerate(((s_hbm, s), (tab_hbm, tab), (w_hbm, w), (d_hbm, d)))
    ]
    for copy in in_copies:
        copy.start()

    barrier = pltpu.get_barrier_semaphore()

    def greet(i, carry):
        @pl.when(i != row)
        def _():
            pl.semaphore_signal(barrier, inc=1, device_id={"row": i}, device_id_type=pl.DeviceIdType.MESH)
        return carry

    lax.fori_loop(0, DEVS, greet, 0)
    pl.semaphore_signal(barrier, inc=1, device_id={"coil": 1 - coil}, device_id_type=pl.DeviceIdType.MESH)
    pl.semaphore_signal(barrier, inc=1, device_id={"frame": 1 - frame}, device_id_type=pl.DeviceIdType.MESH)

    for q in range(4):
        u_copies[q].wait()
        p, top = q // 2, (q % 2) * 16
        for half in range(2):
            total = jnp.zeros((16, 512), F32)
            for k in range(RANK):
                total += v_ref[frame, k] * u[p, k, top:top + 16, half * 512:(half + 1) * 512].astype(F32)
            f[p, top:top + 16, half * 512:(half + 1) * 512] = total

    in_copies[0].wait()
    in_copies[1].wait()
    in_copies[2].wait()
    halo_s[...] = jnp.zeros_like(halo_s)
    for p in range(2):
        halo_s[0, p:p + 1, :] = f[p, 0:1, :]
        halo_s[1, p:p + 1, :] = f[p, 31:32, :]
    halo_s[1, 2:3, :] = w[31:32, :]

    def coil_images(c, carry):
        sr = s[0, c].astype(F32)
        si = s[1, c].astype(F32)
        fr, fi = f[0], f[1]
        at = pl.multiple_of((c % PER) * 32, 32)
        a[c // PER, pl.ds(at, 32), :] = (sr * fr - si * fi).astype(BF16)
        a[c // PER, pl.ds(128 + at, 32), :] = (sr * fi + si * fr).astype(BF16)
        return carry

    lax.fori_loop(0, COILS, coil_images, 0)

    pl.semaphore_wait(barrier, DEVS + 1)

    up = pltpu.make_async_remote_copy(
        halo_s.at[0], halo_r.at[1], halo_send.at[0], halo_recv.at[1],
        device_id={"row": (row + DEVS - 1) % DEVS}, device_id_type=pl.DeviceIdType.MESH)
    down = pltpu.make_async_remote_copy(
        halo_s.at[1], halo_r.at[0], halo_send.at[1], halo_recv.at[0],
        device_id={"row": (row + 1) % DEVS}, device_id_type=pl.DeviceIdType.MESH)
    up.start()
    down.start()

    def send_eight(src, dst, send_sem, recv_sem, g, jj):
        for k in range(8):
            to = jj * 8 + k
            rows = pl.ds(pl.multiple_of(to * 32, 32), 32)
            mine = pl.ds(pl.multiple_of(row * 32, 32), 32)

            @pl.when(to != row)
            def _():
                pltpu.make_async_remote_copy(
                    src.at[g, rows], dst.at[g, mine], send_sem.at[g], recv_sem.at[g],
                    device_id={"row": to}, device_id_type=pl.DeviceIdType.MESH).start()

            @pl.when(to == row)
            def _():
                dst[g, mine, :] = src[g, mine, :]

    def wait_all(ref, sem, g):
        view = ref.at[g, pl.ds(0, N - 32)]
        pltpu.make_async_copy(view, view, sem.at[g]).wait()

    def forward_x(q, carry):
        g, step = q // 4, q % 4
        jj = (my_y + step) % 4
        cols = pl.ds(pl.multiple_of(jj * 256, 256), 256)
        lhs = a[g]
        c_part = dot(lhs, tab[0, :, cols])
        s_part = dot(lhs, tab[1, :, cols])
        both = (c_part[:128] + s_part[128:], c_part[128:] - s_part[:128])
        for p in range(2):
            for h in range(2):
                w4 = swap_blocks([both[p][c * 32:(c + 1) * 32, h * 128:(h + 1) * 128] for c in range(4)])
                for i in range(4):
                    at = pl.multiple_of((jj * 8 + h * 4 + i) * 32, 32)
                    x[g, pl.ds(at, 32), p * 128:(p + 1) * 128] = w4[i].astype(BF16)
        send_eight(x, land, x_send, x_recv, g, jj)
        return carry

    lax.fori_loop(0, 8, forward_x, 0)

    in_copies[3].wait()
    mask_rows = jnp.broadcast_to(mask_ref[...].astype(F32), (128, N))
    mcol[...] = mask_rows.T

    def turn(q, carry):
        g, p = q // 2, q % 2
        block = d[p, 0, pl.ds(g * PER, PER)].reshape(128, N).astype(F32)
        lanes = pl.ds(pl.multiple_of(p * 128, 128), 128)
        dt[g, :, lanes] = block.T.astype(BF16)
        return carry

    lax.fori_loop(0, 4, turn, 0)

    up.wait()
    down.wait()
    lane = lax.broadcasted_iota(jnp.int32, (ROWS, N), 1)
    line = lax.broadcasted_iota(jnp.int32, (ROWS, N), 0)
    last_col = lane == N - 1
    last_line = line == ROWS - 1
    across, downs = [], []
    for p in range(2):
        cur = f[p]
        across.append(jnp.where(last_col, 0.0, pltpu.roll(cur, N - 1, 1) - cur))
        below = jnp.where(last_line, halo_r[1, p:p + 1, :], pltpu.roll(cur, ROWS - 1, 0))
        downs.append(jnp.where(last_line & (row == DEVS - 1), 0.0, below - cur))
    scale = w[...] / jnp.sqrt(across[0] * across[0] + across[1] * across[1]
                              + downs[0] * downs[0] + downs[1] * downs[1] + TV_EPS)
    above = halo_r[0]
    top_across = jnp.where(lax.broadcasted_iota(jnp.int32, (8, N), 1) == N - 1, 0.0, pltpu.roll(above, N - 1, 1) - above)
    top_down = [f[p, 0:1, :] - above[p:p + 1] for p in range(2)]
    top_scale = above[2:3] / jnp.sqrt(top_across[0:1] * top_across[0:1] + top_across[1:2] * top_across[1:2]
                                      + top_down[0] * top_down[0] + top_down[1] * top_down[1] + TV_EPS)
    for p in range(2):
        fa = scale * across[p]
        fd = scale * downs[p]
        top = jnp.where(row == 0, 0.0, top_scale * top_down[p])
        left = jnp.where(lane == 0, 0.0, pltpu.roll(fa, 1, 1))
        over = jnp.where(line == 0, top, pltpu.roll(fd, 1, 0))
        tvg[p] = TV_GAIN * ((left - fa) + (over - fd))

    def middle(g, carry):
        wait_all(land, x_recv, g)

        def residual(kt, inner):
            rows = pl.ds(pl.multiple_of(kt * 256, 256), 256)
            c_part = dot(tab[0, rows, :], land[g])
            s_part = dot(tab[1, rows, :], land[g])
            keep = mcol[rows, :]
            real = c_part[:, :128] + s_part[:, 128:] - dt[g, rows, :128].astype(F32)
            imag = c_part[:, 128:] - s_part[:, :128] - dt[g, rows, 128:].astype(F32)
            mis[rows, :128] = (keep * real).astype(BF16)
            mis[rows, 128:] = (keep * imag).astype(BF16)
            return inner

        lax.fori_loop(0, 4, residual, 0)

        def back(step, inner):
            jj = (my_y + step) % 4
            rows = pl.ds(pl.multiple_of(jj * 256, 256), 256)
            c_part = dot(tab[0, rows, :], mis[...])
            s_part = dot(tab[1, rows, :], mis[...])
            b[g, rows, :128] = (c_part[:, :128] - s_part[:, 128:]).astype(BF16)
            b[g, rows, 128:] = (c_part[:, 128:] + s_part[:, :128]).astype(BF16)
            send_eight(b, r, b_send, b_recv, g, jj)
            return inner

        lax.fori_loop(0, 4, back, 0)
        return carry

    lax.fori_loop(0, GROUPS, middle, 0)

    for g in range(GROUPS):
        wait_all(r, b_recv, g)

        def gather(j, carry):
            lanes = pl.ds(pl.multiple_of(j * 128, 128), 128)
            for p in range(2):
                got = swap_blocks([
                    r[g, pl.ds(pl.multiple_of((4 * j + i) * 32, 32), 32), p * 128:(p + 1) * 128].astype(F32)
                    for i in range(4)])
                for c in range(4):
                    lmat[p * 128 + c * 32:p * 128 + (c + 1) * 32, lanes] = got[c].astype(BF16)
            return carry

        lax.fori_loop(0, 8, gather, 0)

        def inverse_x(xt, carry):
            cols = pl.ds(pl.multiple_of(xt * 256, 256), 256)
            lhs = lmat[...]
            c_part = dot(lhs, tab[0, :, cols])
            s_part = dot(lhs, tab[1, :, cols])
            real = c_part[:128] - s_part[128:]
            imag = c_part[128:] + s_part[:128]
            gr = jnp.zeros((32, 256), F32)
            gi = jnp.zeros((32, 256), F32)
            for c in range(PER):
                sr = s[0, g * PER + c, :, cols].astype(F32)
                si = s[1, g * PER + c, :, cols].astype(F32)
                br = real[c * 32:(c + 1) * 32]
                bi = imag[c * 32:(c + 1) * 32]
                gr += sr * br + si * bi
                gi += sr * bi - si * br
            if g == 0:
                acc[0, :, cols] = gr
                acc[1, :, cols] = gi
            else:
                part_s[xt, 0] = (acc[0, :, cols] + gr).astype(BF16)
                part_s[xt, 1] = (acc[1, :, cols] + gi).astype(BF16)
                pltpu.make_async_remote_copy(
                    part_s.at[xt], part_r.at[xt], p_send.at[xt], p_recv.at[xt],
                    device_id={"coil": 1 - coil}, device_id_type=pl.DeviceIdType.MESH).start()
            return carry

        lax.fori_loop(0, 4, inverse_x, 0)

    def finish(xt, carry):
        pltpu.make_async_copy(part_r.at[xt], part_r.at[xt], p_recv.at[xt]).wait()
        cols = pl.ds(pl.multiple_of(xt * 256, 256), 256)
        for p in range(2):
            whole = part_s[xt, p].astype(F32) + part_r[xt, p].astype(F32) + tvg[p, :, cols]
            comb[frame, xt, p] = whole
        pltpu.make_async_remote_copy(
            comb.at[frame, xt], comb.at[frame, xt], c_send.at[xt], c_recv.at[xt],
            device_id={"frame": 1 - frame}, device_id_type=pl.DeviceIdType.MESH).start()
        return carry

    lax.fori_loop(0, 4, finish, 0)
    for xt in range(4):
        pltpu.make_async_copy(comb.at[1 - frame, xt], comb.at[1 - frame, xt], c_recv.at[xt]).wait()
        pltpu.make_async_copy(comb.at[frame, xt], comb.at[frame, xt], c_send.at[xt]).wait()
        pltpu.make_async_copy(part_s.at[xt], part_s.at[xt], p_send.at[xt]).wait()
        for t in range(2):
            for p in range(2):
                out_ref[t, p, :, xt * 256:(xt + 1) * 256] = comb[t, xt, p]
    for g in range(GROUPS):
        wait_all(x, x_send, g)
        wait_all(b, b_send, g)


def outer_kernel(v_ref, g_ref, out_ref):
    block = pl.program_id(1)
    first = g_ref[0, 0]
    second = g_ref[1, 0]
    for k in range(out_ref.shape[1]):
        at = block * out_ref.shape[1] + k
        out_ref[0, k] = v_ref[0, at] * first + v_ref[1, at] * second


def shards(factor_u, temporal_v, sensitivity, kspace_data, sample_mask, tv_weight):
    table = jnp.asarray(fourier_tables())
    v = temporal_v.astype(F32)
    anywhere = pl.BlockSpec(memory_space=pl.ANY)
    dma = pltpu.SemaphoreType.DMA
    combined = pl.pallas_call(
        main_kernel,
        out_shape=jax.ShapeDtypeStruct((2, 2, ROWS, N), F32),
        in_specs=[
            pl.BlockSpec(memory_space=pltpu.SMEM), pl.BlockSpec(memory_space=pltpu.VMEM),
            anywhere, anywhere, anywhere, anywhere, anywhere,
        ],
        out_specs=pl.BlockSpec(memory_space=pltpu.VMEM),
        scratch_shapes=[
            pltpu.VMEM((2, RANK, ROWS, N), BF16),
            pltpu.VMEM((2, COILS, ROWS, N), BF16),
            pltpu.VMEM((2, 1, COILS, ROWS, N), BF16),
            pltpu.VMEM((ROWS, N), F32),
            pltpu.VMEM((2, N, N), BF16),
            pltpu.VMEM((2, ROWS, N), F32),
            pltpu.VMEM((GROUPS, 256, N), BF16),
            pltpu.VMEM((GROUPS, N, 256), BF16),
            pltpu.VMEM((N, 128), F32),
            pltpu.VMEM((GROUPS, N, 256), BF16),
            pltpu.VMEM((GROUPS, N, 256), BF16),
            pltpu.VMEM((N, 256), BF16),
            pltpu.VMEM((GROUPS, N, 256), BF16),
            pltpu.VMEM((GROUPS, N, 256), BF16),
            pltpu.VMEM((256, N), BF16),
            pltpu.VMEM((2, ROWS, N), F32),
            pltpu.VMEM((2, 8, N), F32),
            pltpu.VMEM((2, 8, N), F32),
            pltpu.VMEM((4, 2, ROWS, 256), BF16),
            pltpu.VMEM((4, 2, ROWS, 256), BF16),
            pltpu.VMEM((2, 4, 2, ROWS, 256), F32),
            pltpu.VMEM((2, ROWS, N), F32),
            dma((4,)), dma((4,)), dma((2,)), dma((2,)),
            dma((GROUPS,)), dma((GROUPS,)), dma((GROUPS,)), dma((GROUPS,)),
            dma((4,)), dma((4,)), dma((4,)), dma((4,)),
        ],
        compiler_params=pltpu.CompilerParams(
            collective_id=0, has_side_effects=True, vmem_limit_bytes=48 * 1024 * 1024
        ),
        cost_estimate=pl.CostEstimate(flops=9 * 10**9, bytes_accessed=14 * 10**6, transcendentals=40000),
        name="frame_gradient",
    )(v, sample_mask, factor_u, sensitivity, kspace_data, tv_weight, table)
    step = 12
    return pl.pallas_call(
        outer_kernel,
        out_shape=jax.ShapeDtypeStruct((2, RANK, ROWS, N), F32),
        grid=(2, RANK // step),
        in_specs=[
            pl.BlockSpec(memory_space=pltpu.SMEM),
            pl.BlockSpec((2, 1, ROWS, N), lambda p, k: (0, p, 0, 0)),
        ],
        out_specs=pl.BlockSpec((1, step, ROWS, N), lambda p, k: (p, k, 0, 0)),
        compiler_params=pltpu.CompilerParams(vmem_limit_bytes=24 * 1024 * 1024),
        cost_estimate=pl.CostEstimate(flops=10**7, bytes_accessed=13 * 10**6, transcendentals=0),
        name="spread_over_rank",
    )(v, combined)


def solution(mesh):
    return jax.shard_map(
        shards,
        mesh=mesh,
        in_specs=(
            P(None, None, "row", None),
            P(),
            P(None, "coil", "row", None),
            P(None, "frame", "coil", "row", None),
            P("frame", None),
            P("row", None),
        ),
        out_specs=P(None, None, "row", None),
        check_vma=False,
    )
```

```python
import math

import jax
import jax.numpy as jnp
import numpy as np
from jax import lax
from jax.experimental import pallas as pl
from jax.experimental.pallas import tpu as pltpu
from jax.sharding import PartitionSpec as P

N = 1024
ROWS = 32
RANK = 48
COILS = 8
GROUPS = 2
PER = COILS // GROUPS
DEVS = 32
VMEM_LIMIT = 64 * 1024 * 1024 - 640 * 1024
TV_EPS = 0.25
TV_GAIN = 0.5
F32 = jnp.float32
BF16 = jnp.bfloat16


def angle_pair(product):
    angle = 2.0 * math.pi * (product % N) / N
    return np.cos(angle) / math.sqrt(N), np.sin(angle) / math.sqrt(N)


def x_table():
    at = np.arange(N)
    return np.concatenate(angle_pair(at[:, None] * at[None, :])).astype(jnp.bfloat16)


def y_tables():
    quarter = np.arange(N // 4)
    sides = []
    for q in range(4):
        cosine, sine = angle_pair((4 * quarter[:, None] + q) * quarter[None, :])
        sides.append((np.concatenate([cosine, sine], axis=1), np.concatenate([cosine.T, sine.T], axis=1)))
    return np.stack([np.stack([side[k] for side in sides]) for k in range(2)]).astype(jnp.bfloat16)


def swap_blocks(parts):
    lane = lax.broadcasted_iota(jnp.int32, parts[0].shape, 1)
    even = (lane // 32) % 2 == 0
    low = lane < 64
    a = list(parts)
    for x, y in ((0, 1), (2, 3)):
        first = jnp.where(even, a[x], pltpu.roll(a[y], 32, 1))
        second = jnp.where(even, pltpu.roll(a[x], 96, 1), a[y])
        a[x], a[y] = first, second
    for x, y in ((0, 2), (1, 3)):
        first = jnp.where(low, a[x], pltpu.roll(a[y], 64, 1))
        second = jnp.where(low, pltpu.roll(a[x], 64, 1), a[y])
        a[x], a[y] = first, second
    return a


def dot(a, b):
    return jnp.dot(a, b, preferred_element_type=F32)


def main_kernel(
    v_hbm, mask_hbm, u_hbm, s_hbm, d_hbm, w_hbm, xtab_hbm, ytab_hbm, out_ref,
    u, s, d, w, xtab, ytab, mask_ref, v_ref, vcol, f, a, dt, dturn, mcol, mturn, x, land, uq, mis, bq, b, r, lmat, acc, halo_s, halo_r, part_s, part_r, comb, tvg,
    u_sem, in_sem, halo_send, halo_recv, x_send, x_recv, b_send, b_recv, p_send, p_recv, c_send, c_recv,
):
    row = lax.axis_index("row")
    frame = lax.axis_index("frame")
    coil = lax.axis_index("coil")
    my_y = row // 8

    in_copies = []
    names = ((v_hbm, v_ref), (s_hbm, s), (w_hbm, w), (xtab_hbm, xtab), (mask_hbm, mask_ref), (d_hbm, d), (ytab_hbm, ytab))
    for q, (src, dst) in enumerate(names):
        in_copies.append(pltpu.make_async_copy(src, dst, in_sem.at[q]))
    v_in, s_in, w_in, xtab_in, mask_in, d_in, ytab_in = in_copies
    u_copies = []
    for q in range(4):
        part = (q // 2, slice(None), pl.ds((q % 2) * 16, 16))
        u_copies.append(pltpu.make_async_copy(u_hbm.at[part], u.at[part], u_sem.at[q]))
    v_in.start()
    for copy in u_copies + in_copies[1:]:
        copy.start()

    barrier = pltpu.get_barrier_semaphore()

    def greet(i, carry):
        @pl.when(i != row)
        def _():
            pl.semaphore_signal(barrier, inc=1, device_id={"row": i}, device_id_type=pl.DeviceIdType.MESH)
        return carry

    lax.fori_loop(0, DEVS, greet, 0)
    pl.semaphore_signal(barrier, inc=1, device_id={"coil": 1 - coil}, device_id_type=pl.DeviceIdType.MESH)
    pl.semaphore_signal(barrier, inc=1, device_id={"frame": 1 - frame}, device_id_type=pl.DeviceIdType.MESH)

    v_in.wait()
    spread_column(v_ref[...].astype(F32), frame, vcol)
    for q in range(4):
        u_copies[q].wait()
        p, top = q // 2, (q % 2) * 16
        for half in range(2):
            total = jnp.zeros((16, 512), F32)
            for k in range(RANK):
                total += vcol[k:k + 1, :] * u[p, k, top:top + 16, half * 512:(half + 1) * 512].astype(F32)
            f[p, top:top + 16, half * 512:(half + 1) * 512] = total

    s_in.wait()
    w_in.wait()
    halo_s[...] = jnp.zeros_like(halo_s)
    for p in range(2):
        halo_s[0, p:p + 1, :] = f[p, 0:1, :]
        halo_s[1, p:p + 1, :] = f[p, 31:32, :]
    halo_s[1, 2:3, :] = w[31:32, :]

    def coil_images(c, carry):
        sr = s[0, c].astype(F32)
        si = s[1, c].astype(F32)
        fr, fi = f[0], f[1]
        at = pl.multiple_of((c % PER) * 32, 32)
        real = (sr * fr - si * fi).astype(BF16)
        imag = (sr * fi + si * fr).astype(BF16)
        a[c // PER, pl.ds(at, 32), :N] = real
        a[c // PER, pl.ds(at, 32), N:] = imag
        a[c // PER, pl.ds(128 + at, 32), :N] = imag
        a[c // PER, pl.ds(128 + at, 32), N:] = -real
        return carry

    lax.fori_loop(0, COILS, coil_images, 0)
    xtab_in.wait()

    pl.semaphore_wait(barrier, DEVS + 1)

    up = pltpu.make_async_remote_copy(
        halo_s.at[0], halo_r.at[1], halo_send.at[0], halo_recv.at[1],
        device_id={"row": (row + DEVS - 1) % DEVS}, device_id_type=pl.DeviceIdType.MESH)
    down = pltpu.make_async_remote_copy(
        halo_s.at[1], halo_r.at[0], halo_send.at[1], halo_recv.at[0],
        device_id={"row": (row + 1) % DEVS}, device_id_type=pl.DeviceIdType.MESH)
    up.start()
    down.start()

    def send_rows(src, dst, send_sem, recv_sem, g, to):
        rows = pl.ds(pl.multiple_of(to * 32, 32), 32)
        mine = pl.ds(pl.multiple_of(row * 32, 32), 32)

        @pl.when(to != row)
        def _():
            pltpu.make_async_remote_copy(
                src.at[g, rows], dst.at[g, mine], send_sem.at[g], recv_sem.at[g],
                device_id={"row": to}, device_id_type=pl.DeviceIdType.MESH).start()

        @pl.when(to == row)
        def _():
            dst[g, mine, :] = src[g, mine, :]

    def wait_all(ref, sem, g):
        view = ref.at[g, pl.ds(0, N - 32)]
        pltpu.make_async_copy(view, view, sem.at[g]).wait()

    def forward_x(q, carry):
        g, step = q // 4, q % 4
        jj = (my_y + step) % 4
        cols = pl.ds(pl.multiple_of(jj * 256, 256), 256)
        both = dot(a[g], xtab[:, cols])
        for p in range(2):
            for h in range(2):
                w4 = swap_blocks([both[p * 128 + c * 32:p * 128 + (c + 1) * 32, h * 128:(h + 1) * 128] for c in range(4)])
                for i in range(4):
                    at = pl.multiple_of((jj * 8 + h * 4 + i) * 32, 32)
                    x[g, pl.ds(at, 32), p * 128:(p + 1) * 128] = w4[i].astype(BF16)
        for k in range(8):
            send_rows(x, land, x_send, x_recv, g, jj * 8 + k)
        return carry

    lax.fori_loop(0, 8, forward_x, 0)

    d_in.wait()
    mask_in.wait()
    mturn[...] = jnp.broadcast_to(mask_ref[...].astype(F32), (128, N)).T
    for q in range(4):
        mcol[q] = mturn[pl.ds(q, 256, stride=4), :]

    def turn(k, carry):
        g, p = k // 2, k % 2
        block = d[p, 0, pl.ds(g * PER, PER)].reshape(128, N).astype(F32)
        dturn[...] = block.T
        for q in range(4):
            dt[g, p, q] = dturn[pl.ds(q, 256, stride=4), :].astype(BF16)
        return carry

    lax.fori_loop(0, 4, turn, 0)
    ytab_in.wait()

    up.wait()
    down.wait()
    lane = lax.broadcasted_iota(jnp.int32, (ROWS, N), 1)
    line = lax.broadcasted_iota(jnp.int32, (ROWS, N), 0)
    last_col = lane == N - 1
    last_line = line == ROWS - 1
    across, downs = [], []
    for p in range(2):
        cur = f[p]
        across.append(jnp.where(last_col, 0.0, pltpu.roll(cur, N - 1, 1) - cur))
        below = jnp.where(last_line, halo_r[1, p:p + 1, :], pltpu.roll(cur, ROWS - 1, 0))
        downs.append(jnp.where(last_line & (row == DEVS - 1), 0.0, below - cur))
    scale = w[...] / jnp.sqrt(across[0] * across[0] + across[1] * across[1]
                              + downs[0] * downs[0] + downs[1] * downs[1] + TV_EPS)
    above = halo_r[0]
    top_across = jnp.where(lax.broadcasted_iota(jnp.int32, (8, N), 1) == N - 1, 0.0, pltpu.roll(above, N - 1, 1) - above)
    top_down = [f[p, 0:1, :] - above[p:p + 1] for p in range(2)]
    top_scale = above[2:3] / jnp.sqrt(top_across[0:1] * top_across[0:1] + top_across[1:2] * top_across[1:2]
                                      + top_down[0] * top_down[0] + top_down[1] * top_down[1] + TV_EPS)
    for p in range(2):
        fa = scale * across[p]
        fd = scale * downs[p]
        top = jnp.where(row == 0, 0.0, top_scale * top_down[p])
        left = jnp.where(lane == 0, 0.0, pltpu.roll(fa, 1, 1))
        over = jnp.where(line == 0, top, pltpu.roll(fd, 1, 0))
        tvg[p] = TV_GAIN * ((left - fa) + (over - fd))

    def middle(g, carry):
        wait_all(land, x_recv, g)

        def spread(k, inner):
            part = [land[g, pl.ds(pl.multiple_of(p * 256 + k * 32, 32), 32), :].astype(F32) for p in range(4)]
            at = pl.multiple_of(k * 32, 32)
            plus, minus = part[0] + part[2], part[0] - part[2]
            other, cross = part[1] + part[3], part[1] - part[3]
            turned = jnp.concatenate([cross[:, 128:], -cross[:, :128]], axis=1)
            for q, value in enumerate((plus + other, minus + turned, plus - other, minus - turned)):
                short = value.astype(BF16)
                uq[q, pl.ds(at, 32), :] = short
                uq[q, pl.ds(256 + at, 32), :128] = short[:, 128:]
                uq[q, pl.ds(256 + at, 32), 128:] = -short[:, :128]
            return inner

        lax.fori_loop(0, 8, spread, 0)
        for q in range(4):
            spectrum = dot(ytab[0, q], uq[q])
            keep = mcol[q]
            real = (keep * (spectrum[:, :128] - dt[g, 0, q].astype(F32))).astype(BF16)
            imag = (keep * (spectrum[:, 128:] - dt[g, 1, q].astype(F32))).astype(BF16)
            mis[q, :256, :128] = real
            mis[q, :256, 128:] = imag
            mis[q, 256:, :128] = -imag
            mis[q, 256:, 128:] = real
        for q in range(4):
            bq[q] = dot(ytab[1, q], mis[q])

        def back(k, inner):
            at = pl.ds(pl.multiple_of(k * 32, 32), 32)
            part = [bq[q, at, :] for q in range(4)]
            plus, minus = part[0] + part[2], part[0] - part[2]
            other, cross = part[1] + part[3], part[1] - part[3]
            turned = jnp.concatenate([-cross[:, 128:], cross[:, :128]], axis=1)
            for p, value in enumerate((plus + other, minus + turned, plus - other, minus - turned)):
                to = pl.multiple_of(p * 256 + k * 32, 32)
                b[g, pl.ds(to, 32), :] = value.astype(BF16)
                send_rows(b, r, b_send, b_recv, g, p * 8 + k)
            return inner

        def back_from(k, inner):
            return back((row + k) % 8, inner)

        lax.fori_loop(0, 8, back_from, 0)
        return carry

    lax.fori_loop(0, GROUPS, middle, 0)

    for g in range(GROUPS):
        wait_all(r, b_recv, g)

        def gather(j, carry):
            lanes = pl.ds(pl.multiple_of(j * 128, 128), 128)
            for p in range(2):
                got = swap_blocks([
                    r[g, pl.ds(pl.multiple_of((4 * j + i) * 32, 32), 32), p * 128:(p + 1) * 128].astype(F32)
                    for i in range(4)])
                for c in range(4):
                    short = got[c].astype(BF16)
                    other = pl.ds(pl.multiple_of(N + j * 128, 128), 128)
                    line = slice(c * 32, (c + 1) * 32)
                    cross = slice(128 + c * 32, 128 + (c + 1) * 32)
                    if p == 0:
                        lmat[line, lanes] = short
                        lmat[cross, other] = short
                    else:
                        lmat[line, other] = -short
                        lmat[cross, lanes] = short
            return carry

        lax.fori_loop(0, 8, gather, 0)

        def inverse_x(xt, carry):
            cols = pl.ds(pl.multiple_of(xt * 256, 256), 256)
            both = dot(lmat[...], xtab[:, cols])
            real, imag = both[:128], both[128:]
            gr = jnp.zeros((32, 256), F32)
            gi = jnp.zeros((32, 256), F32)
            for c in range(PER):
                sr = s[0, g * PER + c, :, cols].astype(F32)
                si = s[1, g * PER + c, :, cols].astype(F32)
                br = real[c * 32:(c + 1) * 32]
                bi = imag[c * 32:(c + 1) * 32]
                gr += sr * br + si * bi
                gi += sr * bi - si * br
            if g == 0:
                acc[0, :, cols] = gr
                acc[1, :, cols] = gi
            else:
                part_s[xt, 0] = (acc[0, :, cols] + gr).astype(BF16)
                part_s[xt, 1] = (acc[1, :, cols] + gi).astype(BF16)
                pltpu.make_async_remote_copy(
                    part_s.at[xt], part_r.at[xt], p_send.at[xt], p_recv.at[xt],
                    device_id={"coil": 1 - coil}, device_id_type=pl.DeviceIdType.MESH).start()
            return carry

        lax.fori_loop(0, 4, inverse_x, 0)

    def finish(xt, carry):
        pltpu.make_async_copy(part_r.at[xt], part_r.at[xt], p_recv.at[xt]).wait()
        cols = pl.ds(pl.multiple_of(xt * 256, 256), 256)
        for p in range(2):
            whole = part_s[xt, p].astype(F32) + part_r[xt, p].astype(F32) + tvg[p, :, cols]
            comb[frame, xt, p] = whole
        pltpu.make_async_remote_copy(
            comb.at[frame, xt], comb.at[frame, xt], c_send.at[xt], c_recv.at[xt],
            device_id={"frame": 1 - frame}, device_id_type=pl.DeviceIdType.MESH).start()
        return carry

    lax.fori_loop(0, 4, finish, 0)
    for xt in range(4):
        pltpu.make_async_copy(comb.at[1 - frame, xt], comb.at[1 - frame, xt], c_recv.at[xt]).wait()
        pltpu.make_async_copy(comb.at[frame, xt], comb.at[frame, xt], c_send.at[xt]).wait()
        pltpu.make_async_copy(part_s.at[xt], part_s.at[xt], p_send.at[xt]).wait()
        for t in range(2):
            for p in range(2):
                out_ref[t, p, :, xt * 256:(xt + 1) * 256] = comb[t, xt, p]
    for g in range(GROUPS):
        wait_all(x, x_send, g)
        wait_all(b, b_send, g)


def spread_column(values, which, column):
    line = jnp.where(which == 0, values[0:1], values[1:2])
    here = lax.broadcasted_iota(jnp.int32, (RANK, RANK), 0) == lax.broadcasted_iota(jnp.int32, (RANK, RANK), 1)
    column[...] = dot(jnp.where(here, line, 0.0).astype(BF16), jnp.ones((RANK, column.shape[1]), BF16))


def outer_kernel(v_hbm, g_hbm, out_hbm, v_ref, g_ref, first, second, out, in_sem, sem):
    g_in = [pltpu.make_async_copy(g_hbm.at[:, p], g_ref.at[:, p], in_sem.at[p]) for p in range(2)]
    v_in = pltpu.make_async_copy(v_hbm, v_ref, in_sem.at[2])
    v_in.start()
    for copy in g_in:
        copy.start()
    v_in.wait()
    values = v_ref[...].astype(F32)
    spread_column(values, 0, first)
    spread_column(values, 1, second)
    step = 4
    for p in range(2):
        g_in[p].wait()

        def some(block, carry):
            for top in range(0, ROWS, 8):
                for half in range(0, N, 512):
                    part = (slice(top, top + 8), slice(half, half + 512))
                    g0 = g_ref[0, p, part[0], part[1]]
                    g1 = g_ref[1, p, part[0], part[1]]
                    for k in range(step):
                        at = block * step + k
                        out[p, at, part[0], part[1]] = first[pl.ds(at, 1), :] * g0 + second[pl.ds(at, 1), :] * g1
            ranks = pl.ds(block * step, step)
            pltpu.make_async_copy(out.at[p, ranks], out_hbm.at[p, ranks], sem).start()
            return carry

        lax.fori_loop(0, RANK // step, some, 0)
    pltpu.make_async_copy(out, out_hbm, sem).wait()


def shards(factor_u, temporal_v, sensitivity, kspace_data, sample_mask, tv_weight):
    anywhere = pl.BlockSpec(memory_space=pltpu.HBM)
    dma = pltpu.SemaphoreType.DMA
    combined = pl.pallas_call(
        main_kernel,
        out_shape=jax.ShapeDtypeStruct((2, 2, ROWS, N), F32),
        in_specs=[anywhere] * 8,
        out_specs=pl.BlockSpec(memory_space=pltpu.VMEM),
        scratch_shapes=[
            pltpu.VMEM((2, RANK, ROWS, N), BF16),
            pltpu.VMEM((2, COILS, ROWS, N), BF16),
            pltpu.VMEM((2, 1, COILS, ROWS, N), BF16),
            pltpu.VMEM((ROWS, N), F32),
            pltpu.VMEM((2 * N, N), BF16),
            pltpu.VMEM((2, 4, 256, 512), BF16),
            pltpu.VMEM((1, N), jnp.int32),
            pltpu.VMEM((2, RANK), BF16),
            pltpu.VMEM((RANK, 512), F32),
            pltpu.VMEM((2, ROWS, N), F32),
            pltpu.VMEM((GROUPS, 256, 2 * N), BF16),
            pltpu.VMEM((GROUPS, 2, 4, 256, 128), BF16),
            pltpu.VMEM((N, 128), F32),
            pltpu.VMEM((4, 256, 128), F32),
            pltpu.VMEM((N, 128), F32),
            pltpu.VMEM((GROUPS, N, 256), BF16),
            pltpu.VMEM((GROUPS, N, 256), BF16),
            pltpu.VMEM((4, 512, 256), BF16),
            pltpu.VMEM((4, 512, 256), BF16),
            pltpu.VMEM((4, 256, 256), F32),
            pltpu.VMEM((GROUPS, N, 256), BF16),
            pltpu.VMEM((GROUPS, N, 256), BF16),
            pltpu.VMEM((256, 2 * N), BF16),
            pltpu.VMEM((2, ROWS, N), F32),
            pltpu.VMEM((2, 8, N), F32),
            pltpu.VMEM((2, 8, N), F32),
            pltpu.VMEM((4, 2, ROWS, 256), BF16),
            pltpu.VMEM((4, 2, ROWS, 256), BF16),
            pltpu.VMEM((2, 4, 2, ROWS, 256), F32),
            pltpu.VMEM((2, ROWS, N), F32),
            dma((4,)), dma((7,)), dma((2,)), dma((2,)),
            dma((GROUPS,)), dma((GROUPS,)), dma((GROUPS,)), dma((GROUPS,)),
            dma((4,)), dma((4,)), dma((4,)), dma((4,)),
        ],
        compiler_params=pltpu.CompilerParams(
            collective_id=0, has_side_effects=True, vmem_limit_bytes=VMEM_LIMIT
        ),
        cost_estimate=pl.CostEstimate(flops=6 * 10**9, bytes_accessed=14 * 10**6, transcendentals=40000),
        name="frame_gradient",
    )(temporal_v, sample_mask, factor_u, sensitivity, kspace_data, tv_weight, jnp.asarray(x_table()), jnp.asarray(y_tables()))
    return pl.pallas_call(
        outer_kernel,
        out_shape=jax.ShapeDtypeStruct((2, RANK, ROWS, N), F32),
        in_specs=[anywhere] * 2,
        out_specs=anywhere,
        scratch_shapes=[
            pltpu.VMEM((2, RANK), BF16), pltpu.VMEM((2, 2, ROWS, N), F32),
            pltpu.VMEM((RANK, 512), F32), pltpu.VMEM((RANK, 512), F32),
            pltpu.VMEM((2, RANK, ROWS, N), F32), dma((3,)), dma,
        ],
        compiler_params=pltpu.CompilerParams(vmem_limit_bytes=VMEM_LIMIT),
        cost_estimate=pl.CostEstimate(flops=10**7, bytes_accessed=13 * 10**6, transcendentals=0),
        name="spread_over_rank",
    )(temporal_v, combined)


def solution(mesh):
    return jax.shard_map(
        shards,
        mesh=mesh,
        in_specs=(
            P(None, None, "row", None),
            P(),
            P(None, "coil", "row", None),
            P(None, "frame", "coil", "row", None),
            P("frame", None),
            P("row", None),
        ),
        out_specs=P(None, None, "row", None),
        check_vma=False,
    )
```

```python
import math

import jax
import jax.numpy as jnp
import numpy as np
from jax import lax
from jax.experimental import pallas as pl
from jax.experimental.pallas import tpu as pltpu
from jax.sharding import PartitionSpec as P

N = 1024
ROWS = 32
RANK = 48
COILS = 8
GROUPS = 2
PER = COILS // GROUPS
DEVS = 32
VMEM_LIMIT = 64 * 1024 * 1024 - 640 * 1024
TV_EPS = 0.25
TV_GAIN = 0.5
F32 = jnp.float32
BF16 = jnp.bfloat16


def angle_pair(product):
    angle = 2.0 * math.pi * (product % N) / N
    return np.cos(angle) / math.sqrt(N), np.sin(angle) / math.sqrt(N)


def x_table():
    at = np.arange(N)
    return np.concatenate(angle_pair(at[:, None] * at[None, :])).astype(jnp.bfloat16)


def y_tables():
    quarter = np.arange(N // 4)
    sides = []
    for q in range(4):
        cosine, sine = angle_pair((4 * quarter[:, None] + q) * quarter[None, :])
        sides.append((np.concatenate([cosine, sine], axis=1), np.concatenate([cosine.T, sine.T], axis=1)))
    return np.stack([np.stack([side[k] for side in sides]) for k in range(2)]).astype(jnp.bfloat16)


def swap_blocks(parts):
    lane = lax.broadcasted_iota(jnp.int32, parts[0].shape, 1)
    even = (lane // 32) % 2 == 0
    low = lane < 64
    a = list(parts)
    for x, y in ((0, 1), (2, 3)):
        first = jnp.where(even, a[x], pltpu.roll(a[y], 32, 1))
        second = jnp.where(even, pltpu.roll(a[x], 96, 1), a[y])
        a[x], a[y] = first, second
    for x, y in ((0, 2), (1, 3)):
        first = jnp.where(low, a[x], pltpu.roll(a[y], 64, 1))
        second = jnp.where(low, pltpu.roll(a[x], 64, 1), a[y])
        a[x], a[y] = first, second
    return a


def dot(a, b):
    return jnp.dot(a, b, preferred_element_type=F32)


def main_kernel(
    v_hbm, mask_hbm, u_hbm, s_hbm, d_hbm, w_hbm, xtab_hbm, ytab_hbm, out_ref,
    u, s, d, w, xtab, ytab, mask_ref, v_ref, vcol, f, fs, fl, fy, dturn, mcol, x, land, uq, mis, bq, b, r,
    gacc, gs, gl, lmat, acc, halo_s, halo_r, part_s, part_r, comb, tvg,
    u_sem, in_sem, halo_send, halo_recv, s_send, s_recv, e_send, e_recv, f_send, f_recv, b_send, b_recv,
    g_send, g_recv, p_send, p_recv, c_send, c_recv,
):
    row = lax.axis_index("row")
    frame = lax.axis_index("frame")
    coil = lax.axis_index("coil")

    names = ((v_hbm, v_ref), (s_hbm, s), (mask_hbm, mask_ref), (d_hbm, d), (ytab_hbm, ytab), (w_hbm, w), (xtab_hbm, xtab))
    in_copies = [pltpu.make_async_copy(src, dst, in_sem.at[q]) for q, (src, dst) in enumerate(names)]
    v_in, s_in, mask_in, d_in, ytab_in, w_in, xtab_in = in_copies
    u_copies = []
    for q in range(4):
        part = (q // 2, slice(None), pl.ds((q % 2) * 16, 16))
        u_copies.append(pltpu.make_async_copy(u_hbm.at[part], u.at[part], u_sem.at[q]))
    for copy in in_copies[:2] + u_copies + in_copies[2:]:
        copy.start()

    barrier = pltpu.get_barrier_semaphore()

    def greet(i, carry):
        @pl.when(i != row)
        def _():
            pl.semaphore_signal(barrier, inc=1, device_id={"row": i}, device_id_type=pl.DeviceIdType.MESH)
        return carry

    lax.fori_loop(0, DEVS, greet, 0)
    pl.semaphore_signal(barrier, inc=1, device_id={"coil": 1 - coil}, device_id_type=pl.DeviceIdType.MESH)
    pl.semaphore_signal(barrier, inc=1, device_id={"frame": 1 - frame}, device_id_type=pl.DeviceIdType.MESH)

    def send_rows(src, dst, send_sem, recv_sem, size, to):
        rows = pl.ds(pl.multiple_of(to * size, size), size)
        mine = pl.ds(pl.multiple_of(row * size, size), size)

        @pl.when(to != row)
        def _():
            pltpu.make_async_remote_copy(
                src.at[rows], dst.at[mine], send_sem, recv_sem,
                device_id={"row": to}, device_id_type=pl.DeviceIdType.MESH).start()

        @pl.when(to == row)
        def _():
            dst[mine, :] = src[rows, :]

    def wait_bytes(ref, sem):
        pltpu.make_async_copy(ref, ref, sem).wait()

    def wait_all(ref, sem):
        wait_bytes(ref.at[pl.ds(0, ref.shape[0] // DEVS * (DEVS - 1))], sem)

    s_in.wait()

    def lay_maps(k, carry):
        j = (row // 4 + k) % 8
        lanes = pl.ds(pl.multiple_of(j * 128, 128), 128)
        for p in range(2):
            w4 = swap_blocks([s[p, frame * PER + c, :, lanes].astype(F32) for c in range(4)])
            for i in range(4):
                x[pl.ds(pl.multiple_of((j * 4 + i) * 32, 32), 32), p * 128:(p + 1) * 128] = w4[i].astype(BF16)
        return carry

    def send_maps(k, carry):
        send_rows(x, land.at[frame], s_send.at[0], s_recv.at[0], 32, (row + k) % DEVS)
        return carry

    lax.fori_loop(0, 8, lay_maps, 0)
    pl.semaphore_wait(barrier, DEVS + 1)
    lax.fori_loop(0, DEVS, send_maps, 0)

    v_in.wait()
    spread_column(v_ref[...].astype(F32), frame, vcol)
    for q in range(4):
        u_copies[q].wait()
        p, top = q // 2, (q % 2) * 16
        for half in range(2):
            total = jnp.zeros((16, 512), F32)
            for k in range(RANK):
                total += vcol[k:k + 1, :] * u[p, k, top:top + 16, half * 512:(half + 1) * 512].astype(F32)
            f[p, top:top + 16, half * 512:(half + 1) * 512] = total

    def send_frame(k, carry):
        j = (row // 4 + k) % 8
        lanes = pl.ds(pl.multiple_of(j * 128, 128), 128)
        w4 = swap_blocks([f[hp % 2, hp // 2 * 16:hp // 2 * 16 + 16, lanes] for hp in range(4)])
        for i in range(4):
            to = j * 4 + i
            fs[pl.ds(pl.multiple_of(to * 16, 16), 16), :] = w4[i].astype(BF16)
            send_rows(fs, fl, f_send.at[0], f_recv.at[0], 16, to)
        return carry

    lax.fori_loop(0, 8, send_frame, 0)

    w_in.wait()
    halo_s[...] = jnp.zeros_like(halo_s)
    for p in range(2):
        halo_s[0, p:p + 1, :] = f[p, 0:1, :]
        halo_s[1, p:p + 1, :] = f[p, 31:32, :]
    halo_s[1, 2:3, :] = w[31:32, :]
    up = pltpu.make_async_remote_copy(
        halo_s.at[0], halo_r.at[1], halo_send.at[0], halo_recv.at[1],
        device_id={"row": (row + DEVS - 1) % DEVS}, device_id_type=pl.DeviceIdType.MESH)
    down = pltpu.make_async_remote_copy(
        halo_s.at[1], halo_r.at[0], halo_send.at[1], halo_recv.at[0],
        device_id={"row": (row + 1) % DEVS}, device_id_type=pl.DeviceIdType.MESH)
    up.start()
    down.start()

    d_in.wait()
    mask_in.wait()
    ytab_in.wait()

    def fold_back(at):
        part = [bq[q, at, :] for q in range(4)]
        plus, minus = part[0] + part[2], part[0] - part[2]
        other, cross = part[1] + part[3], part[1] - part[3]
        turned = jnp.concatenate([-cross[:, 128:], cross[:, :128]], axis=1)
        return plus + other, minus + turned, plus - other, minus - turned

    def measured(g, carry):
        keep = -mask_ref[...].astype(F32)
        for p in range(2):
            dturn[...] = (d[p, 0, pl.ds(g * PER, PER)].reshape(128, N).astype(F32) * keep).T
            for q in range(4):
                value = dturn[pl.ds(q, 256, stride=4), :].astype(BF16)
                if p == 0:
                    mis[q, :256, :128] = value
                    mis[q, 256:, 128:] = value
                else:
                    mis[q, :256, 128:] = value
                    mis[q, 256:, :128] = -value
        for q in range(4):
            bq[q] = dot(ytab[1, q], mis[q])

        def back(k, inner):
            turn = (row + k) % 8
            for p, value in enumerate(fold_back(pl.ds(pl.multiple_of(turn * 32, 32), 32))):
                b[g, pl.ds(pl.multiple_of(p * 256 + turn * 32, 32), 32), :] = value.astype(BF16)
                send_rows(b.at[g], r.at[g], b_send.at[g], b_recv.at[g], 32, p * 8 + turn)
            return inner

        lax.fori_loop(0, 8, back, 0)
        return carry

    lax.fori_loop(0, GROUPS, measured, 0)

    dturn[...] = jnp.broadcast_to(mask_ref[...].astype(F32), (128, N)).T
    for q in range(4):
        mcol[q] = dturn[pl.ds(q, 256, stride=4), :]
    up.wait()
    down.wait()
    lane = lax.broadcasted_iota(jnp.int32, (ROWS, N), 1)
    line = lax.broadcasted_iota(jnp.int32, (ROWS, N), 0)
    last_col = lane == N - 1
    last_line = line == ROWS - 1
    across, downs = [], []
    for p in range(2):
        cur = f[p]
        across.append(jnp.where(last_col, 0.0, pltpu.roll(cur, N - 1, 1) - cur))
        below = jnp.where(last_line, halo_r[1, p:p + 1, :], pltpu.roll(cur, ROWS - 1, 0))
        downs.append(jnp.where(last_line & (row == DEVS - 1), 0.0, below - cur))
    scale = w[...] / jnp.sqrt(across[0] * across[0] + across[1] * across[1]
                              + downs[0] * downs[0] + downs[1] * downs[1] + TV_EPS)
    above = halo_r[0]
    top_across = jnp.where(lax.broadcasted_iota(jnp.int32, (8, N), 1) == N - 1, 0.0, pltpu.roll(above, N - 1, 1) - above)
    top_down = [f[p, 0:1, :] - above[p:p + 1] for p in range(2)]
    top_scale = above[2:3] / jnp.sqrt(top_across[0:1] * top_across[0:1] + top_across[1:2] * top_across[1:2]
                                      + top_down[0] * top_down[0] + top_down[1] * top_down[1] + TV_EPS)
    for p in range(2):
        fa = scale * across[p]
        fd = scale * downs[p]
        top = jnp.where(row == 0, 0.0, top_scale * top_down[p])
        left = jnp.where(lane == 0, 0.0, pltpu.roll(fa, 1, 1))
        over = jnp.where(line == 0, top, pltpu.roll(fd, 1, 0))
        tvg[p] = TV_GAIN * ((left - fa) + (over - fd))

    wait_all(land.at[frame], s_recv.at[0])
    share = pltpu.make_async_remote_copy(
        land.at[frame], land.at[frame], e_send.at[0], e_recv.at[0],
        device_id={"frame": 1 - frame}, device_id_type=pl.DeviceIdType.MESH)
    share.start()
    wait_all(fl, f_recv.at[0])
    source = lax.broadcasted_iota(jnp.int32, (128, 512), 0)
    target = lax.broadcasted_iota(jnp.int32, (128, 512), 1)
    same = (source // 32 == target // 128) & (source % 32 == target % 32)
    copies = jnp.where(same, 1.0, 0.0).astype(BF16)
    fy[...] = dot(fl[...], copies)

    def pencil(turn_g, carry):
        g = (frame + turn_g) % 2

        @pl.when(turn_g == 1)
        def _():
            wait_bytes(land.at[1 - frame], e_recv.at[0])

        def spread(k, inner):
            part = []
            for p in range(4):
                at = p * 8 + k
                maps = land[g, pl.ds(pl.multiple_of(at * 32, 32), 32), :].astype(F32)
                image = fy[pl.ds(pl.multiple_of(at * 16, 16), 16), :]
                fr = jnp.concatenate([image[:, :128], image[:, 256:384]], axis=0)
                fi = jnp.concatenate([image[:, 128:256], image[:, 384:]], axis=0)
                sr, si = maps[:, :128], maps[:, 128:]
                part.append((sr * fr - si * fi, sr * fi + si * fr))
            plus = [part[0][z] + part[2][z] for z in range(2)]
            minus = [part[0][z] - part[2][z] for z in range(2)]
            other = [part[1][z] + part[3][z] for z in range(2)]
            cross = [part[1][z] - part[3][z] for z in range(2)]
            values = (
                (plus[0] + other[0], plus[1] + other[1]),
                (minus[0] + cross[1], minus[1] - cross[0]),
                (plus[0] - other[0], plus[1] - other[1]),
                (minus[0] - cross[1], minus[1] + cross[0]),
            )
            at = pl.multiple_of(k * 32, 32)
            for q, (real, imag) in enumerate(values):
                real, imag = real.astype(BF16), imag.astype(BF16)
                uq[q, pl.ds(at, 32), :128] = real
                uq[q, pl.ds(at, 32), 128:] = imag
                uq[q, pl.ds(256 + at, 32), :128] = imag
                uq[q, pl.ds(256 + at, 32), 128:] = -real
            return inner

        lax.fori_loop(0, 8, spread, 0)
        for q in range(4):
            spectrum = dot(ytab[0, q], uq[q])
            keep = mcol[q]
            real = (keep * spectrum[:, :128]).astype(BF16)
            imag = (keep * spectrum[:, 128:]).astype(BF16)
            mis[q, :256, :128] = real
            mis[q, :256, 128:] = imag
            mis[q, 256:, :128] = -imag
            mis[q, 256:, 128:] = real
        for q in range(4):
            bq[q] = dot(ytab[1, q], mis[q])

        def collect(k, inner):
            turn = (row + k) % 8
            for p, value in enumerate(fold_back(pl.ds(pl.multiple_of(turn * 32, 32), 32))):
                to = p * 8 + turn
                rows = pl.ds(pl.multiple_of(to * 32, 32), 32)
                maps = land[g, rows, :].astype(F32)
                sr, si = maps[:, :128], maps[:, 128:]
                ar, ai = value[:, :128], value[:, 128:]
                gr = sr * ar + si * ai
                gi = sr * ai - si * ar

                @pl.when(turn_g == 0)
                def _():
                    gacc[rows, :128] = gr
                    gacc[rows, 128:] = gi

                @pl.when(turn_g == 1)
                def _():
                    whole = []
                    for z in (gacc[rows, :128] + gr, gacc[rows, 128:] + gi):
                        z = z + pltpu.roll(z, 64, 1)
                        whole.append(z + pltpu.roll(z, 32, 1))
                    block = lax.broadcasted_iota(jnp.int32, (16, 128), 1) // 32
                    upper = jnp.where(block == 0, whole[0][:16], whole[1][:16])
                    lower = jnp.where(block == 2, whole[0][16:], whole[1][16:])
                    gs[pl.ds(pl.multiple_of(to * 16, 16), 16), :] = jnp.where(block < 2, upper, lower).astype(BF16)
                    send_rows(gs, gl, g_send.at[0], g_recv.at[0], 16, to)
            return inner

        lax.fori_loop(0, 8, collect, 0)
        return carry

    lax.fori_loop(0, 2, pencil, 0)

    xtab_in.wait()
    for g in range(GROUPS):
        wait_all(r.at[g], b_recv.at[g])

        def gather(j, carry):
            lanes = pl.ds(pl.multiple_of(j * 128, 128), 128)
            for p in range(2):
                got = swap_blocks([
                    r[g, pl.ds(pl.multiple_of((4 * j + i) * 32, 32), 32), p * 128:(p + 1) * 128].astype(F32)
                    for i in range(4)])
                for c in range(4):
                    short = got[c].astype(BF16)
                    other = pl.ds(pl.multiple_of(N + j * 128, 128), 128)
                    line = slice(c * 32, (c + 1) * 32)
                    cross = slice(128 + c * 32, 128 + (c + 1) * 32)
                    if p == 0:
                        lmat[line, lanes] = short
                        lmat[cross, other] = short
                    else:
                        lmat[line, other] = -short
                        lmat[cross, lanes] = short
            return carry

        lax.fori_loop(0, 8, gather, 0)

        if g == GROUPS - 1:
            wait_all(gl, g_recv.at[0])

            def unpack(j, carry):
                lanes = pl.ds(pl.multiple_of(j * 128, 128), 128)
                got = swap_blocks([
                    gl[pl.ds(pl.multiple_of((4 * j + i) * 16, 16), 16), :].astype(F32) for i in range(4)])
                for hp in range(4):
                    acc[hp % 2, hp // 2 * 16:hp // 2 * 16 + 16, lanes] += got[hp]
                return carry

            lax.fori_loop(0, 8, unpack, 0)

        def inverse_x(xt, carry):
            cols = pl.ds(pl.multiple_of(xt * 256, 256), 256)
            both = dot(lmat[...], xtab[:, cols])
            real, imag = both[:128], both[128:]
            gr = jnp.zeros((32, 256), F32)
            gi = jnp.zeros((32, 256), F32)
            for c in range(PER):
                sr = s[0, g * PER + c, :, cols].astype(F32)
                si = s[1, g * PER + c, :, cols].astype(F32)
                br = real[c * 32:(c + 1) * 32]
                bi = imag[c * 32:(c + 1) * 32]
                gr += sr * br + si * bi
                gi += sr * bi - si * br
            if g == 0:
                acc[0, :, cols] = gr
                acc[1, :, cols] = gi
            else:
                part_s[xt, 0] = (acc[0, :, cols] + gr).astype(BF16)
                part_s[xt, 1] = (acc[1, :, cols] + gi).astype(BF16)
                pltpu.make_async_remote_copy(
                    part_s.at[xt], part_r.at[xt], p_send.at[xt], p_recv.at[xt],
                    device_id={"coil": 1 - coil}, device_id_type=pl.DeviceIdType.MESH).start()
            return carry

        lax.fori_loop(0, 4, inverse_x, 0)

    def finish(xt, carry):
        wait_bytes(part_r.at[xt], p_recv.at[xt])
        cols = pl.ds(pl.multiple_of(xt * 256, 256), 256)
        for p in range(2):
            comb[frame, xt, p] = part_s[xt, p].astype(F32) + part_r[xt, p].astype(F32) + tvg[p, :, cols]
        pltpu.make_async_remote_copy(
            comb.at[frame, xt], comb.at[frame, xt], c_send.at[xt], c_recv.at[xt],
            device_id={"frame": 1 - frame}, device_id_type=pl.DeviceIdType.MESH).start()
        return carry

    lax.fori_loop(0, 4, finish, 0)
    for xt in range(4):
        wait_bytes(comb.at[1 - frame, xt], c_recv.at[xt])
        for t in range(2):
            for p in range(2):
                out_ref[t, p, :, xt * 256:(xt + 1) * 256] = comb[t, xt, p]
    for xt in range(4):
        wait_bytes(comb.at[frame, xt], c_send.at[xt])
        wait_bytes(part_s.at[xt], p_send.at[xt])
    wait_all(x, s_send.at[0])
    wait_all(fs, f_send.at[0])
    wait_all(gs, g_send.at[0])
    share.wait_send()
    for g in range(GROUPS):
        wait_all(b.at[g], b_send.at[g])


def spread_column(values, which, column):
    line = jnp.where(which == 0, values[0:1], values[1:2])
    here = lax.broadcasted_iota(jnp.int32, (RANK, RANK), 0) == lax.broadcasted_iota(jnp.int32, (RANK, RANK), 1)
    column[...] = dot(jnp.where(here, line, 0.0).astype(BF16), jnp.ones((RANK, column.shape[1]), BF16))


def outer_kernel(v_hbm, g_hbm, out_hbm, v_ref, g_ref, first, second, out, in_sem, sem):
    g_in = [pltpu.make_async_copy(g_hbm.at[:, p], g_ref.at[:, p], in_sem.at[p]) for p in range(2)]
    v_in = pltpu.make_async_copy(v_hbm, v_ref, in_sem.at[2])
    v_in.start()
    for copy in g_in:
        copy.start()
    v_in.wait()
    values = v_ref[...].astype(F32)
    spread_column(values, 0, first)
    spread_column(values, 1, second)
    step = 4
    for p in range(2):
        g_in[p].wait()

        def some(block, carry):
            for top in range(0, ROWS, 8):
                for half in range(0, N, 512):
                    part = (slice(top, top + 8), slice(half, half + 512))
                    g0 = g_ref[0, p, part[0], part[1]]
                    g1 = g_ref[1, p, part[0], part[1]]
                    for k in range(step):
                        at = block * step + k
                        out[p, at, part[0], part[1]] = first[pl.ds(at, 1), :] * g0 + second[pl.ds(at, 1), :] * g1
            ranks = pl.ds(block * step, step)
            pltpu.make_async_copy(out.at[p, ranks], out_hbm.at[p, ranks], sem).start()
            return carry

        lax.fori_loop(0, RANK // step, some, 0)
    pltpu.make_async_copy(out, out_hbm, sem).wait()


def shards(factor_u, temporal_v, sensitivity, kspace_data, sample_mask, tv_weight):
    anywhere = pl.BlockSpec(memory_space=pltpu.HBM)
    dma = pltpu.SemaphoreType.DMA
    combined = pl.pallas_call(
        main_kernel,
        out_shape=jax.ShapeDtypeStruct((2, 2, ROWS, N), F32),
        in_specs=[anywhere] * 8,
        out_specs=pl.BlockSpec(memory_space=pltpu.VMEM),
        scratch_shapes=[
            pltpu.VMEM((2, RANK, ROWS, N), BF16),
            pltpu.VMEM((2, COILS, ROWS, N), BF16),
            pltpu.VMEM((2, 1, COILS, ROWS, N), BF16),
            pltpu.VMEM((ROWS, N), F32),
            pltpu.VMEM((2 * N, N), BF16),
            pltpu.VMEM((2, 4, 256, 512), BF16),
            pltpu.VMEM((1, N), jnp.int32),
            pltpu.VMEM((2, RANK), BF16),
            pltpu.VMEM((RANK, 512), F32),
            pltpu.VMEM((2, ROWS, N), F32),
            pltpu.VMEM((N // 2, 128), BF16),
            pltpu.VMEM((N // 2, 128), BF16),
            pltpu.VMEM((N // 2, 512), F32),
            pltpu.VMEM((N, 128), F32),
            pltpu.VMEM((4, 256, 128), F32),
            pltpu.VMEM((N, 256), BF16),
            pltpu.VMEM((GROUPS, N, 256), BF16),
            pltpu.VMEM((4, 512, 256), BF16),
            pltpu.VMEM((4, 512, 256), BF16),
            pltpu.VMEM((4, 256, 256), F32),
            pltpu.VMEM((GROUPS, N, 256), BF16),
            pltpu.VMEM((GROUPS, N, 256), BF16),
            pltpu.VMEM((N, 256), F32),
            pltpu.VMEM((N // 2, 128), BF16),
            pltpu.VMEM((N // 2, 128), BF16),
            pltpu.VMEM((256, 2 * N), BF16),
            pltpu.VMEM((2, ROWS, N), F32),
            pltpu.VMEM((2, 8, N), F32),
            pltpu.VMEM((2, 8, N), F32),
            pltpu.VMEM((4, 2, ROWS, 256), BF16),
            pltpu.VMEM((4, 2, ROWS, 256), BF16),
            pltpu.VMEM((2, 4, 2, ROWS, 256), F32),
            pltpu.VMEM((2, ROWS, N), F32),
            dma((4,)), dma((7,)), dma((2,)), dma((2,)),
            dma((1,)), dma((1,)), dma((1,)), dma((1,)), dma((1,)), dma((1,)), dma((GROUPS,)), dma((GROUPS,)),
            dma((1,)), dma((1,)), dma((4,)), dma((4,)), dma((4,)), dma((4,)),
        ],
        compiler_params=pltpu.CompilerParams(
            collective_id=0, has_side_effects=True, vmem_limit_bytes=VMEM_LIMIT
        ),
        cost_estimate=pl.CostEstimate(flops=6 * 10**9, bytes_accessed=14 * 10**6, transcendentals=40000),
        name="frame_gradient",
    )(temporal_v, sample_mask, factor_u, sensitivity, kspace_data, tv_weight, jnp.asarray(x_table()), jnp.asarray(y_tables()))
    return pl.pallas_call(
        outer_kernel,
        out_shape=jax.ShapeDtypeStruct((2, RANK, ROWS, N), F32),
        in_specs=[anywhere] * 2,
        out_specs=anywhere,
        scratch_shapes=[
            pltpu.VMEM((2, RANK), BF16), pltpu.VMEM((2, 2, ROWS, N), F32),
            pltpu.VMEM((RANK, 512), F32), pltpu.VMEM((RANK, 512), F32),
            pltpu.VMEM((2, RANK, ROWS, N), F32), dma((3,)), dma,
        ],
        compiler_params=pltpu.CompilerParams(vmem_limit_bytes=VMEM_LIMIT),
        cost_estimate=pl.CostEstimate(flops=10**7, bytes_accessed=13 * 10**6, transcendentals=0),
        name="spread_over_rank",
    )(temporal_v, combined)


def solution(mesh):
    return jax.shard_map(
        shards,
        mesh=mesh,
        in_specs=(
            P(None, None, "row", None),
            P(),
            P(None, "coil", "row", None),
            P(None, "frame", "coil", "row", None),
            P("frame", None),
            P("row", None),
        ),
        out_specs=P(None, None, "row", None),
        check_vma=False,
    )
```

```python
import math

import jax
import jax.numpy as jnp
import numpy as np
from jax import lax
from jax.experimental import pallas as pl
from jax.experimental.pallas import tpu as pltpu
from jax.sharding import PartitionSpec as P

N = 1024
ROWS = 32
RANK = 48
COILS = 8
GROUPS = 2
PER = COILS // GROUPS
DEVS = 32
VMEM_LIMIT = 64 * 1024 * 1024 - 640 * 1024
TV_EPS = 0.25
TV_GAIN = 0.5
F32 = jnp.float32
BF16 = jnp.bfloat16


def angle_pair(product):
    angle = 2.0 * math.pi * (product % N) / N
    return np.cos(angle) / math.sqrt(N), np.sin(angle) / math.sqrt(N)


def x_table():
    at = np.arange(N)
    return np.concatenate(angle_pair(at[:, None] * at[None, :])).astype(jnp.bfloat16)


def y_tables():
    quarter = np.arange(N // 4)
    sides = []
    for q in range(4):
        cosine, sine = angle_pair((4 * quarter[:, None] + q) * quarter[None, :])
        sides.append((np.concatenate([cosine, sine], axis=1), np.concatenate([cosine.T, sine.T], axis=1)))
    return np.stack([np.stack([side[k] for side in sides]) for k in range(2)]).astype(jnp.bfloat16)


def swap_blocks(parts):
    lane = lax.broadcasted_iota(jnp.int32, parts[0].shape, 1)
    even = (lane // 32) % 2 == 0
    low = lane < 64
    a = list(parts)
    for x, y in ((0, 1), (2, 3)):
        first = jnp.where(even, a[x], pltpu.roll(a[y], 32, 1))
        second = jnp.where(even, pltpu.roll(a[x], 96, 1), a[y])
        a[x], a[y] = first, second
    for x, y in ((0, 2), (1, 3)):
        first = jnp.where(low, a[x], pltpu.roll(a[y], 64, 1))
        second = jnp.where(low, pltpu.roll(a[x], 64, 1), a[y])
        a[x], a[y] = first, second
    return a


def dot(a, b):
    return jnp.dot(a, b, preferred_element_type=F32)


def main_kernel(
    v_hbm, mask_hbm, u_hbm, s_hbm, d_hbm, w_hbm, xtab_hbm, ytab_hbm, out_hbm,
    u, s, d, w, xtab, ytab, mask_ref, v_ref, vcol, f, fs, fl, fy, dturn, mcol, x, land, uq, mis, bq, b, r,
    gacc, gs, gl, lmat, acc, halo_s, halo_r, part_s, part_r, comb, tvg,
    u_sem, in_sem, halo_send, halo_recv, s_send, s_recv, e_send, e_recv, f_send, f_recv, b_send, b_recv,
    g_send, g_recv, p_send, p_recv, c_send, c_recv, o_sem,
):
    row = lax.axis_index("row")
    frame = lax.axis_index("frame")
    coil = lax.axis_index("coil")

    names = ((v_hbm, v_ref), (s_hbm, s), (mask_hbm, mask_ref), (d_hbm, d), (ytab_hbm, ytab), (w_hbm, w), (xtab_hbm, xtab))
    in_copies = [pltpu.make_async_copy(src, dst, in_sem.at[q]) for q, (src, dst) in enumerate(names)]
    v_in, s_in, mask_in, d_in, ytab_in, w_in, xtab_in = in_copies
    u_copies = []
    for q in range(4):
        part = (q // 2, slice(None), pl.ds((q % 2) * 16, 16))
        u_copies.append(pltpu.make_async_copy(u_hbm.at[part], u.at[part], u_sem.at[q]))
    for copy in in_copies[:2] + u_copies + in_copies[2:]:
        copy.start()

    barrier = pltpu.get_barrier_semaphore()

    def greet(i, carry):
        @pl.when(i != row)
        def _():
            pl.semaphore_signal(barrier, inc=1, device_id={"row": i}, device_id_type=pl.DeviceIdType.MESH)
        return carry

    lax.fori_loop(0, DEVS, greet, 0)
    pl.semaphore_signal(barrier, inc=1, device_id={"coil": 1 - coil}, device_id_type=pl.DeviceIdType.MESH)
    pl.semaphore_signal(barrier, inc=1, device_id={"frame": 1 - frame}, device_id_type=pl.DeviceIdType.MESH)

    def send_all(src, dst, send_sem, recv_sem, size):
        mine = pl.ds(pl.multiple_of(row * size, size), size)

        def send(k, carry):
            to = (row + 13 * k) % DEVS
            pltpu.make_async_remote_copy(
                src.at[pl.ds(pl.multiple_of(to * size, size), size)], dst.at[mine], send_sem, recv_sem,
                device_id={"row": to}, device_id_type=pl.DeviceIdType.MESH).start()
            return carry

        lax.fori_loop(1, DEVS, send, 0)
        dst[mine, :] = src[mine, :]

    def wait_bytes(ref, sem):
        pltpu.make_async_copy(ref, ref, sem).wait()

    def wait_all(ref, sem):
        wait_bytes(ref.at[pl.ds(0, ref.shape[0] // DEVS * (DEVS - 1))], sem)

    s_in.wait()

    def lay_maps(k, carry):
        j = k
        lanes = pl.ds(pl.multiple_of(j * 128, 128), 128)
        for p in range(2):
            w4 = swap_blocks([s[p, frame * PER + c, :, lanes] for c in range(4)])
            for i in range(4):
                x[pl.ds(pl.multiple_of((j * 4 + i) * 32, 32), 32), p * 128:(p + 1) * 128] = w4[i]
        return carry

    lax.fori_loop(0, 8, lay_maps, 0)
    pl.semaphore_wait(barrier, DEVS + 1)
    send_all(x, land.at[frame], s_send.at[0], s_recv.at[0], 32)

    v_in.wait()
    spread_column(v_ref[...].astype(F32), frame, vcol)
    for q in range(4):
        u_copies[q].wait()
        p, top = q // 2, (q % 2) * 16
        for half in range(2):
            total = jnp.zeros((16, 512), F32)
            for k in range(RANK):
                total += vcol[k:k + 1, :] * u[p, k, top:top + 16, half * 512:(half + 1) * 512].astype(F32)
            f[p, top:top + 16, half * 512:(half + 1) * 512] = total

    def send_frame(k, carry):
        j = k
        lanes = pl.ds(pl.multiple_of(j * 128, 128), 128)
        w4 = swap_blocks([f[hp % 2, hp // 2 * 16:hp // 2 * 16 + 16, lanes] for hp in range(4)])
        for i in range(4):
            to = j * 4 + i
            fs[pl.ds(pl.multiple_of(to * 16, 16), 16), :] = w4[i].astype(BF16)
        return carry

    lax.fori_loop(0, 8, send_frame, 0)
    send_all(fs, fl, f_send.at[0], f_recv.at[0], 16)

    w_in.wait()
    halo_s[...] = jnp.zeros_like(halo_s)
    for p in range(2):
        halo_s[0, p:p + 1, :] = f[p, 0:1, :]
        halo_s[1, p:p + 1, :] = f[p, 31:32, :]
    halo_s[1, 2:3, :] = w[31:32, :]
    up = pltpu.make_async_remote_copy(
        halo_s.at[0], halo_r.at[1], halo_send.at[0], halo_recv.at[1],
        device_id={"row": (row + DEVS - 1) % DEVS}, device_id_type=pl.DeviceIdType.MESH)
    down = pltpu.make_async_remote_copy(
        halo_s.at[1], halo_r.at[0], halo_send.at[1], halo_recv.at[0],
        device_id={"row": (row + 1) % DEVS}, device_id_type=pl.DeviceIdType.MESH)
    up.start()
    down.start()

    d_in.wait()
    mask_in.wait()
    ytab_in.wait()

    def fold_back(at):
        part = [bq[q, at, :] for q in range(4)]
        plus, minus = part[0] + part[2], part[0] - part[2]
        other, cross = part[1] + part[3], part[1] - part[3]
        turned = jnp.concatenate([-cross[:, 128:], cross[:, :128]], axis=1)
        return plus + other, minus + turned, plus - other, minus - turned

    def measured(g, carry):
        keep = -mask_ref[...].astype(F32)
        for p in range(2):
            dturn[...] = (d[p, 0, pl.ds(g * PER, PER)].reshape(128, N).astype(F32) * keep).T
            for q in range(4):
                value = dturn[pl.ds(q, 256, stride=4), :].astype(BF16)
                if p == 0:
                    mis[q, :256, :128] = value
                    mis[q, 256:, 128:] = value
                else:
                    mis[q, :256, 128:] = value
                    mis[q, 256:, :128] = -value
        for q in range(4):
            bq[q] = dot(ytab[1, q], mis[q])

        def back(k, inner):
            turn = k
            for p, value in enumerate(fold_back(pl.ds(pl.multiple_of(turn * 32, 32), 32))):
                b[g, pl.ds(pl.multiple_of(p * 256 + turn * 32, 32), 32), :] = value.astype(BF16)
            return inner

        lax.fori_loop(0, 8, back, 0)
        return carry

    def send_measured(g):
        mine = pl.ds(pl.multiple_of(row * 32, 32), 32)
        own = pltpu.make_async_copy(b.at[g, mine], r.at[g, mine], b_recv.at[g, row // 4])

        def send(k, carry):
            to = (row + 13 * k) % DEVS
            pltpu.make_async_remote_copy(
                b.at[g, pl.ds(pl.multiple_of(to * 32, 32), 32)], r.at[g, mine], b_send.at[g], b_recv.at[g, row // 4],
                device_id={"row": to}, device_id_type=pl.DeviceIdType.MESH).start()
            return carry

        lax.fori_loop(1, DEVS, send, 0)
        own.start()

    lax.fori_loop(0, GROUPS, measured, 0)
    send_measured(0)

    dturn[...] = jnp.broadcast_to(mask_ref[...].astype(F32), (128, N)).T
    for q in range(4):
        mcol[q] = dturn[pl.ds(q, 256, stride=4), :]
    wait_all(land.at[frame], s_recv.at[0])
    share = pltpu.make_async_remote_copy(
        land.at[frame], land.at[frame], e_send.at[0], e_recv.at[0],
        device_id={"frame": 1 - frame}, device_id_type=pl.DeviceIdType.MESH)
    share.start()
    wait_all(fl, f_recv.at[0])
    send_measured(1)
    source = lax.broadcasted_iota(jnp.int32, (128, 512), 0)
    target = lax.broadcasted_iota(jnp.int32, (128, 512), 1)
    same = (source // 32 == target // 128) & (source % 32 == target % 32)
    copies = jnp.where(same, 1.0, 0.0).astype(BF16)
    fy[...] = dot(fl[...], copies)

    for turn_g in range(2):
        g = (frame + turn_g) % 2
        if turn_g == 1:
            wait_bytes(land.at[1 - frame], e_recv.at[0])

        def spread(k, inner):
            part = []
            for p in range(4):
                at = p * 8 + k
                maps = land[g, pl.ds(pl.multiple_of(at * 32, 32), 32), :].astype(F32)
                image = fy[pl.ds(pl.multiple_of(at * 16, 16), 16), :]
                fr = jnp.concatenate([image[:, :128], image[:, 256:384]], axis=0)
                fi = jnp.concatenate([image[:, 128:256], image[:, 384:]], axis=0)
                sr, si = maps[:, :128], maps[:, 128:]
                part.append((sr * fr - si * fi, sr * fi + si * fr))
            plus = [part[0][z] + part[2][z] for z in range(2)]
            minus = [part[0][z] - part[2][z] for z in range(2)]
            other = [part[1][z] + part[3][z] for z in range(2)]
            cross = [part[1][z] - part[3][z] for z in range(2)]
            values = (
                (plus[0] + other[0], plus[1] + other[1]),
                (minus[0] + cross[1], minus[1] - cross[0]),
                (plus[0] - other[0], plus[1] - other[1]),
                (minus[0] - cross[1], minus[1] + cross[0]),
            )
            at = pl.multiple_of(k * 32, 32)
            for q, (real, imag) in enumerate(values):
                real, imag = real.astype(BF16), imag.astype(BF16)
                uq[q, pl.ds(at, 32), :128] = real
                uq[q, pl.ds(at, 32), 128:] = imag
                uq[q, pl.ds(256 + at, 32), :128] = imag
                uq[q, pl.ds(256 + at, 32), 128:] = -real
            return inner

        lax.fori_loop(0, 8, spread, 0)
        for q in range(4):
            spectrum = dot(ytab[0, q], uq[q])
            keep = mcol[q]
            real = (keep * spectrum[:, :128]).astype(BF16)
            imag = (keep * spectrum[:, 128:]).astype(BF16)
            mis[q, :256, :128] = real
            mis[q, :256, 128:] = imag
            mis[q, 256:, :128] = -imag
            mis[q, 256:, 128:] = real
        for q in range(4):
            bq[q] = dot(ytab[1, q], mis[q])

        def collect(k, inner):
            turn = k
            for p, value in enumerate(fold_back(pl.ds(pl.multiple_of(turn * 32, 32), 32))):
                to = p * 8 + turn
                rows = pl.ds(pl.multiple_of(to * 32, 32), 32)
                maps = land[g, rows, :].astype(F32)
                sr, si = maps[:, :128], maps[:, 128:]
                ar, ai = value[:, :128], value[:, 128:]
                gr = sr * ar + si * ai
                gi = sr * ai - si * ar

                if turn_g == 0:
                    gacc[rows, :128] = gr
                    gacc[rows, 128:] = gi
                else:
                    whole = []
                    for z in (gacc[rows, :128] + gr, gacc[rows, 128:] + gi):
                        z = z + pltpu.roll(z, 64, 1)
                        whole.append(z + pltpu.roll(z, 32, 1))
                    block = lax.broadcasted_iota(jnp.int32, (16, 128), 1) // 32
                    upper = jnp.where(block == 0, whole[0][:16], whole[1][:16])
                    lower = jnp.where(block == 2, whole[0][16:], whole[1][16:])
                    gs[pl.ds(pl.multiple_of(to * 16, 16), 16), :] = jnp.where(block < 2, upper, lower).astype(BF16)
            return inner

        lax.fori_loop(0, 8, collect, 0)
    send_all(gs, gl, g_send.at[0], g_recv.at[0], 16)

    up.wait()
    down.wait()
    lane = lax.broadcasted_iota(jnp.int32, (ROWS, N), 1)
    line = lax.broadcasted_iota(jnp.int32, (ROWS, N), 0)
    last_col = lane == N - 1
    last_line = line == ROWS - 1
    across, downs = [], []
    for p in range(2):
        cur = f[p]
        across.append(jnp.where(last_col, 0.0, pltpu.roll(cur, N - 1, 1) - cur))
        below = jnp.where(last_line, halo_r[1, p:p + 1, :], pltpu.roll(cur, ROWS - 1, 0))
        downs.append(jnp.where(last_line & (row == DEVS - 1), 0.0, below - cur))
    scale = w[...] / jnp.sqrt(across[0] * across[0] + across[1] * across[1]
                              + downs[0] * downs[0] + downs[1] * downs[1] + TV_EPS)
    above = halo_r[0]
    top_across = jnp.where(lax.broadcasted_iota(jnp.int32, (8, N), 1) == N - 1, 0.0, pltpu.roll(above, N - 1, 1) - above)
    top_down = [f[p, 0:1, :] - above[p:p + 1] for p in range(2)]
    top_scale = above[2:3] / jnp.sqrt(top_across[0:1] * top_across[0:1] + top_across[1:2] * top_across[1:2]
                                      + top_down[0] * top_down[0] + top_down[1] * top_down[1] + TV_EPS)
    for p in range(2):
        fa = scale * across[p]
        fd = scale * downs[p]
        top = jnp.where(row == 0, 0.0, top_scale * top_down[p])
        left = jnp.where(lane == 0, 0.0, pltpu.roll(fa, 1, 1))
        over = jnp.where(line == 0, top, pltpu.roll(fd, 1, 0))
        tvg[p] = TV_GAIN * ((left - fa) + (over - fd))

    xtab_in.wait()
    for g in range(GROUPS):

        def gather(k, carry):
            j = (row // 4 + 8 - k) % 8
            wait_bytes(r.at[g, pl.ds(0, 128)], b_recv.at[g, j])
            lanes = pl.ds(pl.multiple_of(j * 128, 128), 128)
            for p in range(2):
                got = swap_blocks([
                    r[g, pl.ds(pl.multiple_of((4 * j + i) * 32, 32), 32), p * 128:(p + 1) * 128]
                    for i in range(4)])
                for c in range(4):
                    short = got[c]
                    other = pl.ds(pl.multiple_of(N + j * 128, 128), 128)
                    line = slice(c * 32, (c + 1) * 32)
                    cross = slice(128 + c * 32, 128 + (c + 1) * 32)
                    if p == 0:
                        lmat[line, lanes] = short
                        lmat[cross, other] = short
                    else:
                        lmat[line, other] = -short
                        lmat[cross, lanes] = short
            return carry

        lax.fori_loop(0, 8, gather, 0)

        def inverse_x(xt, carry):
            cols = pl.ds(pl.multiple_of(xt * 256, 256), 256)
            both = dot(lmat[...], xtab[:, cols])
            real, imag = both[:128], both[128:]
            gr = jnp.zeros((32, 256), F32)
            gi = jnp.zeros((32, 256), F32)
            for c in range(PER):
                sr = s[0, g * PER + c, :, cols].astype(F32)
                si = s[1, g * PER + c, :, cols].astype(F32)
                br = real[c * 32:(c + 1) * 32]
                bi = imag[c * 32:(c + 1) * 32]
                gr += sr * br + si * bi
                gi += sr * bi - si * br
            if g == 0:
                acc[0, :, cols] = gr
                acc[1, :, cols] = gi
            else:
                acc[0, :, cols] += gr
                acc[1, :, cols] += gi
            return carry

        lax.fori_loop(0, 4, inverse_x, 0)

    wait_all(gl, g_recv.at[0])

    def unpack(xt, carry):
        for k in range(2):
            j = 2 * xt + k
            lanes = pl.ds(pl.multiple_of(j * 128, 128), 128)
            got = swap_blocks([gl[pl.ds(pl.multiple_of((4 * j + i) * 16, 16), 16), :] for i in range(4)])
            for hp in range(4):
                p, h = hp % 2, slice(hp // 2 * 16, hp // 2 * 16 + 16)
                part_s[xt, p, h, k * 128:(k + 1) * 128] = (acc[p, h, lanes] + got[hp].astype(F32)).astype(BF16)
        pltpu.make_async_remote_copy(
            part_s.at[xt], part_r.at[xt], p_send.at[xt], p_recv.at[xt],
            device_id={"coil": 1 - coil}, device_id_type=pl.DeviceIdType.MESH).start()
        return carry

    lax.fori_loop(0, 4, unpack, 0)

    def finish(xt, carry):
        wait_bytes(part_r.at[xt], p_recv.at[xt])
        cols = pl.ds(pl.multiple_of(xt * 256, 256), 256)
        for p in range(2):
            comb[frame, xt, p] = part_s[xt, p].astype(F32) + part_r[xt, p].astype(F32) + tvg[p, :, cols]
        pltpu.make_async_remote_copy(
            comb.at[frame, xt], comb.at[frame, xt], c_send.at[xt], c_recv.at[xt],
            device_id={"frame": 1 - frame}, device_id_type=pl.DeviceIdType.MESH).start()
        pltpu.make_async_copy(comb.at[frame, xt], out_hbm.at[frame, xt], o_sem.at[0, xt]).start()
        return carry

    lax.fori_loop(0, 4, finish, 0)
    for xt in range(4):
        wait_bytes(comb.at[1 - frame, xt], c_recv.at[xt])
        pltpu.make_async_copy(comb.at[1 - frame, xt], out_hbm.at[1 - frame, xt], o_sem.at[1, xt]).start()
    for xt in range(4):
        wait_bytes(comb.at[frame, xt], c_send.at[xt])
        wait_bytes(part_s.at[xt], p_send.at[xt])
    wait_all(x, s_send.at[0])
    wait_all(fs, f_send.at[0])
    wait_all(gs, g_send.at[0])
    share.wait_send()
    for k in range(2):
        for xt in range(4):
            wait_bytes(comb.at[frame, xt], o_sem.at[k, xt])
    for g in range(GROUPS):
        wait_all(b.at[g], b_send.at[g])


def spread_column(values, which, column):
    line = jnp.where(which == 0, values[0:1], values[1:2])
    here = lax.broadcasted_iota(jnp.int32, (RANK, RANK), 0) == lax.broadcasted_iota(jnp.int32, (RANK, RANK), 1)
    column[...] = dot(jnp.where(here, line, 0.0).astype(BF16), jnp.ones((RANK, column.shape[1]), BF16))


def outer_kernel(v_hbm, g_hbm, out_hbm, v_ref, g_ref, first, second, out, in_sem, sem):
    g_in = [pltpu.make_async_copy(g_hbm.at[:, :, p], g_ref.at[:, :, p], in_sem.at[p]) for p in range(2)]
    v_in = pltpu.make_async_copy(v_hbm, v_ref, in_sem.at[2])
    v_in.start()
    for copy in g_in:
        copy.start()
    v_in.wait()
    values = v_ref[...].astype(F32)
    spread_column(values, 0, first)
    spread_column(values, 1, second)
    step = 4
    for p in range(2):
        g_in[p].wait()

        def some(block, carry):
            for top in range(0, ROWS, 8):
                for half in range(0, N, 256):
                    part = (slice(top, top + 8), slice(half, half + 256))
                    g0 = g_ref[0, half // 256, p, part[0], :]
                    g1 = g_ref[1, half // 256, p, part[0], :]
                    for k in range(step):
                        at = block * step + k
                        out[p, at, part[0], part[1]] = first[pl.ds(at, 1), :] * g0 + second[pl.ds(at, 1), :] * g1
            ranks = pl.ds(block * step, step)
            pltpu.make_async_copy(out.at[p, ranks], out_hbm.at[p, ranks], sem).start()
            return carry

        lax.fori_loop(0, RANK // step, some, 0)
    pltpu.make_async_copy(out, out_hbm, sem).wait()


def shards(factor_u, temporal_v, sensitivity, kspace_data, sample_mask, tv_weight):
    anywhere = pl.BlockSpec(memory_space=pltpu.HBM)
    dma = pltpu.SemaphoreType.DMA
    combined = pl.pallas_call(
        main_kernel,
        out_shape=jax.ShapeDtypeStruct((2, 4, 2, ROWS, 256), F32),
        in_specs=[anywhere] * 8,
        out_specs=anywhere,
        scratch_shapes=[
            pltpu.VMEM((2, RANK, ROWS, N), BF16),
            pltpu.VMEM((2, COILS, ROWS, N), BF16),
            pltpu.VMEM((2, 1, COILS, ROWS, N), BF16),
            pltpu.VMEM((ROWS, N), F32),
            pltpu.VMEM((2 * N, N), BF16),
            pltpu.VMEM((2, 4, 256, 512), BF16),
            pltpu.VMEM((1, N), jnp.int32),
            pltpu.VMEM((2, RANK), BF16),
            pltpu.VMEM((RANK, 512), F32),
            pltpu.VMEM((2, ROWS, N), F32),
            pltpu.VMEM((N // 2, 128), BF16),
            pltpu.VMEM((N // 2, 128), BF16),
            pltpu.VMEM((N // 2, 512), F32),
            pltpu.VMEM((N, 128), F32),
            pltpu.VMEM((4, 256, 128), F32),
            pltpu.VMEM((N, 256), BF16),
            pltpu.VMEM((GROUPS, N, 256), BF16),
            pltpu.VMEM((4, 512, 256), BF16),
            pltpu.VMEM((4, 512, 256), BF16),
            pltpu.VMEM((4, 256, 256), F32),
            pltpu.VMEM((GROUPS, N, 256), BF16),
            pltpu.VMEM((GROUPS, N, 256), BF16),
            pltpu.VMEM((N, 256), F32),
            pltpu.VMEM((N // 2, 128), BF16),
            pltpu.VMEM((N // 2, 128), BF16),
            pltpu.VMEM((256, 2 * N), BF16),
            pltpu.VMEM((2, ROWS, N), F32),
            pltpu.VMEM((2, 8, N), F32),
            pltpu.VMEM((2, 8, N), F32),
            pltpu.VMEM((4, 2, ROWS, 256), BF16),
            pltpu.VMEM((4, 2, ROWS, 256), BF16),
            pltpu.VMEM((2, 4, 2, ROWS, 256), F32),
            pltpu.VMEM((2, ROWS, N), F32),
            dma((4,)), dma((7,)), dma((2,)), dma((2,)),
            dma((1,)), dma((1,)), dma((1,)), dma((1,)), dma((1,)), dma((1,)), dma((GROUPS,)), dma((GROUPS, 8)),
            dma((1,)), dma((1,)), dma((4,)), dma((4,)), dma((4,)), dma((4,)), dma((2, 4)),
        ],
        compiler_params=pltpu.CompilerParams(
            collective_id=0, has_side_effects=True, vmem_limit_bytes=VMEM_LIMIT
        ),
        cost_estimate=pl.CostEstimate(flops=6 * 10**9, bytes_accessed=14 * 10**6, transcendentals=40000),
        name="frame_gradient",
    )(temporal_v, sample_mask, factor_u, sensitivity, kspace_data, tv_weight, jnp.asarray(x_table()), jnp.asarray(y_tables()))
    return pl.pallas_call(
        outer_kernel,
        out_shape=jax.ShapeDtypeStruct((2, RANK, ROWS, N), F32),
        in_specs=[anywhere] * 2,
        out_specs=anywhere,
        scratch_shapes=[
            pltpu.VMEM((2, RANK), BF16), pltpu.VMEM((2, 4, 2, ROWS, 256), F32),
            pltpu.VMEM((RANK, 256), F32), pltpu.VMEM((RANK, 256), F32),
            pltpu.VMEM((2, RANK, ROWS, N), F32), dma((3,)), dma,
        ],
        compiler_params=pltpu.CompilerParams(vmem_limit_bytes=VMEM_LIMIT),
        cost_estimate=pl.CostEstimate(flops=10**7, bytes_accessed=13 * 10**6, transcendentals=0),
        name="spread_over_rank",
    )(temporal_v, combined)


def solution(mesh):
    return jax.shard_map(
        shards,
        mesh=mesh,
        in_specs=(
            P(None, None, "row", None),
            P(),
            P(None, "coil", "row", None),
            P(None, "frame", "coil", "row", None),
            P("frame", None),
            P("row", None),
        ),
        out_specs=P(None, None, "row", None),
        check_vma=False,
    )
```

```python
import math

import jax
import jax.numpy as jnp
import numpy as np
from jax import lax
from jax.experimental import pallas as pl
from jax.experimental.pallas import tpu as pltpu
from jax.sharding import PartitionSpec as P

N = 1024
ROWS = 32
RANK = 48
COILS = 8
GROUPS = 2
PER = COILS // GROUPS
DEVS = 32
VMEM_LIMIT = 64 * 1024 * 1024 - 640 * 1024
TV_EPS = 0.25
TV_GAIN = 0.5
F32 = jnp.float32
BF16 = jnp.bfloat16


def angle_pair(product):
    angle = 2.0 * math.pi * (product % N) / N
    return np.cos(angle) / math.sqrt(N), np.sin(angle) / math.sqrt(N)


def x_table():
    at = np.arange(N)
    return np.concatenate(angle_pair(at[:, None] * at[None, :])).astype(jnp.bfloat16)


def y_tables():
    quarter = np.arange(N // 4)
    sides = []
    for q in range(4):
        cosine, sine = angle_pair((4 * quarter[:, None] + q) * quarter[None, :])
        sides.append((np.concatenate([cosine, sine], axis=1), np.concatenate([cosine.T, sine.T], axis=1)))
    return np.stack([np.stack([side[k] for side in sides]) for k in range(2)]).astype(jnp.bfloat16)


def swap_blocks(parts):
    lane = lax.broadcasted_iota(jnp.int32, parts[0].shape, 1)
    even = (lane // 32) % 2 == 0
    low = lane < 64
    a = list(parts)
    for x, y in ((0, 1), (2, 3)):
        first = jnp.where(even, a[x], pltpu.roll(a[y], 32, 1))
        second = jnp.where(even, pltpu.roll(a[x], 96, 1), a[y])
        a[x], a[y] = first, second
    for x, y in ((0, 2), (1, 3)):
        first = jnp.where(low, a[x], pltpu.roll(a[y], 64, 1))
        second = jnp.where(low, pltpu.roll(a[x], 64, 1), a[y])
        a[x], a[y] = first, second
    return a


def dot(a, b):
    return jnp.dot(a, b, preferred_element_type=F32)


def main_kernel(
    v_hbm, mask_hbm, u_hbm, s_hbm, d_hbm, w_hbm, xtab_hbm, ytab_hbm, out_hbm,
    u, s, d, w, xtab, ytab, mask_ref, v_ref, vcol, f, fs, fl, fy, dturn, mcol, x, land, uq, mis, bq, b, r,
    gacc, gs, gl, lmat, acc, halo_s, halo_r, part_s, part_r, comb, tvg,
    u_sem, in_sem, halo_send, halo_recv, s_send, s_recv, e_send, e_recv, f_send, f_recv, b_send, b_recv,
    g_send, g_recv, p_send, p_recv, c_send, c_recv, o_sem,
):
    row = lax.axis_index("row")
    frame = lax.axis_index("frame")
    coil = lax.axis_index("coil")

    names = ((v_hbm, v_ref), (s_hbm, s), (mask_hbm, mask_ref), (d_hbm, d), (ytab_hbm, ytab), (w_hbm, w), (xtab_hbm, xtab))
    in_copies = [pltpu.make_async_copy(src, dst, in_sem.at[q]) for q, (src, dst) in enumerate(names)]
    v_in, s_in, mask_in, d_in, ytab_in, w_in, xtab_in = in_copies
    u_copies = []
    for q in range(4):
        part = (q // 2, slice(None), pl.ds((q % 2) * 16, 16))
        u_copies.append(pltpu.make_async_copy(u_hbm.at[part], u.at[part], u_sem.at[q]))
    for copy in in_copies[:2] + u_copies + in_copies[2:]:
        copy.start()

    barrier = pltpu.get_barrier_semaphore()

    def greet(i, carry):
        @pl.when(i != row)
        def _():
            pl.semaphore_signal(barrier, inc=1, device_id={"row": i}, device_id_type=pl.DeviceIdType.MESH)
        return carry

    lax.fori_loop(0, DEVS, greet, 0)
    pl.semaphore_signal(barrier, inc=1, device_id={"coil": 1 - coil}, device_id_type=pl.DeviceIdType.MESH)
    pl.semaphore_signal(barrier, inc=1, device_id={"frame": 1 - frame}, device_id_type=pl.DeviceIdType.MESH)

    def send_all(src, dst, send_sem, recv_sem, size):
        mine = pl.ds(pl.multiple_of(row * size, size), size)

        def send(k, carry):
            to = (row + 13 * k) % DEVS
            pltpu.make_async_remote_copy(
                src.at[pl.ds(pl.multiple_of(to * size, size), size)], dst.at[mine], send_sem, recv_sem,
                device_id={"row": to}, device_id_type=pl.DeviceIdType.MESH).start()
            return carry

        lax.fori_loop(1, DEVS, send, 0)
        dst[mine, :] = src[mine, :]

    def wait_bytes(ref, sem):
        pltpu.make_async_copy(ref, ref, sem).wait()

    def wait_all(ref, sem):
        wait_bytes(ref.at[pl.ds(0, ref.shape[0] // DEVS * (DEVS - 1))], sem)

    s_in.wait()

    def lay_maps(k, carry):
        j = k
        lanes = pl.ds(pl.multiple_of(j * 128, 128), 128)
        for p in range(2):
            w4 = swap_blocks([s[p, frame * PER + c, :, lanes] for c in range(4)])
            for i in range(4):
                x[pl.ds(pl.multiple_of((j * 4 + i) * 32, 32), 32), p * 128:(p + 1) * 128] = w4[i]
        return carry

    lax.fori_loop(0, 8, lay_maps, 0, unroll=8)
    pl.semaphore_wait(barrier, DEVS + 1)
    send_all(x, land.at[frame], s_send.at[0], s_recv.at[0], 32)

    v_in.wait()
    spread_column(v_ref[...].astype(F32), frame, vcol)
    for q in range(4):
        u_copies[q].wait()
        p, top = q // 2, (q % 2) * 16
        for half in range(2):
            total = jnp.zeros((16, 512), F32)
            for k in range(RANK):
                total += vcol[k:k + 1, :] * u[p, k, top:top + 16, half * 512:(half + 1) * 512].astype(F32)
            f[p, top:top + 16, half * 512:(half + 1) * 512] = total

    def send_frame(k, carry):
        j = k
        lanes = pl.ds(pl.multiple_of(j * 128, 128), 128)
        w4 = swap_blocks([f[hp % 2, hp // 2 * 16:hp // 2 * 16 + 16, lanes] for hp in range(4)])
        for i in range(4):
            to = j * 4 + i
            fs[pl.ds(pl.multiple_of(to * 16, 16), 16), :] = w4[i].astype(BF16)
        return carry

    lax.fori_loop(0, 8, send_frame, 0, unroll=4)
    send_all(fs, fl, f_send.at[0], f_recv.at[0], 16)

    w_in.wait()
    halo_s[...] = jnp.zeros_like(halo_s)
    for p in range(2):
        halo_s[0, p:p + 1, :] = f[p, 0:1, :]
        halo_s[1, p:p + 1, :] = f[p, 31:32, :]
    halo_s[1, 2:3, :] = w[31:32, :]
    up = pltpu.make_async_remote_copy(
        halo_s.at[0], halo_r.at[1], halo_send.at[0], halo_recv.at[1],
        device_id={"row": (row + DEVS - 1) % DEVS}, device_id_type=pl.DeviceIdType.MESH)
    down = pltpu.make_async_remote_copy(
        halo_s.at[1], halo_r.at[0], halo_send.at[1], halo_recv.at[0],
        device_id={"row": (row + 1) % DEVS}, device_id_type=pl.DeviceIdType.MESH)
    up.start()
    down.start()

    d_in.wait()
    mask_in.wait()
    ytab_in.wait()

    def fold_back(at):
        part = [bq[q, at, :] for q in range(4)]
        plus, minus = part[0] + part[2], part[0] - part[2]
        other, cross = part[1] + part[3], part[1] - part[3]
        turned = jnp.concatenate([-cross[:, 128:], cross[:, :128]], axis=1)
        return plus + other, minus + turned, plus - other, minus - turned

    def measured(g, carry):
        keep = -mask_ref[...].astype(F32)
        for p in range(2):
            dturn[...] = (d[p, 0, pl.ds(g * PER, PER)].reshape(128, N).astype(F32) * keep).T
            for q in range(4):
                value = dturn[pl.ds(q, 256, stride=4), :].astype(BF16)
                if p == 0:
                    mis[q, :256, :128] = value
                    mis[q, 256:, 128:] = value
                else:
                    mis[q, :256, 128:] = value
                    mis[q, 256:, :128] = -value
        for q in range(4):
            bq[q] = dot(ytab[1, q], mis[q])

        def back(k, inner):
            turn = k
            for p, value in enumerate(fold_back(pl.ds(pl.multiple_of(turn * 32, 32), 32))):
                b[g, pl.ds(pl.multiple_of(p * 256 + turn * 32, 32), 32), :] = value.astype(BF16)
            return inner

        lax.fori_loop(0, 8, back, 0, unroll=2)
        return carry

    def send_measured(g):
        mine = pl.ds(pl.multiple_of(row * 32, 32), 32)
        own = pltpu.make_async_copy(b.at[g, mine], r.at[g, mine], b_recv.at[g, row // 4])

        def send(k, carry):
            to = (row + 13 * k) % DEVS
            pltpu.make_async_remote_copy(
                b.at[g, pl.ds(pl.multiple_of(to * 32, 32), 32)], r.at[g, mine], b_send.at[g], b_recv.at[g, row // 4],
                device_id={"row": to}, device_id_type=pl.DeviceIdType.MESH).start()
            return carry

        lax.fori_loop(1, DEVS, send, 0)
        own.start()

    lax.fori_loop(0, GROUPS, measured, 0)
    send_measured(0)

    dturn[...] = jnp.broadcast_to(mask_ref[...].astype(F32), (128, N)).T
    for q in range(4):
        mcol[q] = dturn[pl.ds(q, 256, stride=4), :]
    wait_all(land.at[frame], s_recv.at[0])
    share = pltpu.make_async_remote_copy(
        land.at[frame], land.at[frame], e_send.at[0], e_recv.at[0],
        device_id={"frame": 1 - frame}, device_id_type=pl.DeviceIdType.MESH)
    share.start()
    wait_all(fl, f_recv.at[0])
    send_measured(1)
    source = lax.broadcasted_iota(jnp.int32, (128, 512), 0)
    target = lax.broadcasted_iota(jnp.int32, (128, 512), 1)
    same = (source // 32 == target // 128) & (source % 32 == target % 32)
    copies = jnp.where(same, 1.0, 0.0).astype(BF16)
    fy[...] = dot(fl[...], copies)

    for turn_g in range(2):
        g = (frame + turn_g) % 2
        if turn_g == 1:
            wait_bytes(land.at[1 - frame], e_recv.at[0])

        def spread(k, inner):
            part = []
            for p in range(4):
                at = p * 8 + k
                maps = land[g, pl.ds(pl.multiple_of(at * 32, 32), 32), :].astype(F32)
                image = fy[pl.ds(pl.multiple_of(at * 16, 16), 16), :]
                fr = jnp.concatenate([image[:, :128], image[:, 256:384]], axis=0)
                fi = jnp.concatenate([image[:, 128:256], image[:, 384:]], axis=0)
                sr, si = maps[:, :128], maps[:, 128:]
                part.append((sr * fr - si * fi, sr * fi + si * fr))
            plus = [part[0][z] + part[2][z] for z in range(2)]
            minus = [part[0][z] - part[2][z] for z in range(2)]
            other = [part[1][z] + part[3][z] for z in range(2)]
            cross = [part[1][z] - part[3][z] for z in range(2)]
            values = (
                (plus[0] + other[0], plus[1] + other[1]),
                (minus[0] + cross[1], minus[1] - cross[0]),
                (plus[0] - other[0], plus[1] - other[1]),
                (minus[0] - cross[1], minus[1] + cross[0]),
            )
            at = pl.multiple_of(k * 32, 32)
            for q, (real, imag) in enumerate(values):
                real, imag = real.astype(BF16), imag.astype(BF16)
                uq[q, pl.ds(at, 32), :128] = real
                uq[q, pl.ds(at, 32), 128:] = imag
                uq[q, pl.ds(256 + at, 32), :128] = imag
                uq[q, pl.ds(256 + at, 32), 128:] = -real
            return inner

        lax.fori_loop(0, 8, spread, 0, unroll=2)
        for q in range(4):
            spectrum = dot(ytab[0, q], uq[q])
            keep = mcol[q]
            real = (keep * spectrum[:, :128]).astype(BF16)
            imag = (keep * spectrum[:, 128:]).astype(BF16)
            mis[q, :256, :128] = real
            mis[q, :256, 128:] = imag
            mis[q, 256:, :128] = -imag
            mis[q, 256:, 128:] = real
        for q in range(4):
            bq[q] = dot(ytab[1, q], mis[q])

        def collect(k, inner):
            turn = k
            for p, value in enumerate(fold_back(pl.ds(pl.multiple_of(turn * 32, 32), 32))):
                to = p * 8 + turn
                rows = pl.ds(pl.multiple_of(to * 32, 32), 32)
                maps = land[g, rows, :].astype(F32)
                sr, si = maps[:, :128], maps[:, 128:]
                ar, ai = value[:, :128], value[:, 128:]
                gr = sr * ar + si * ai
                gi = sr * ai - si * ar

                if turn_g == 0:
                    gacc[rows, :128] = gr
                    gacc[rows, 128:] = gi
                else:
                    whole = []
                    for z in (gacc[rows, :128] + gr, gacc[rows, 128:] + gi):
                        z = z + pltpu.roll(z, 64, 1)
                        whole.append(z + pltpu.roll(z, 32, 1))
                    block = lax.broadcasted_iota(jnp.int32, (16, 128), 1) // 32
                    upper = jnp.where(block == 0, whole[0][:16], whole[1][:16])
                    lower = jnp.where(block == 2, whole[0][16:], whole[1][16:])
                    gs[pl.ds(pl.multiple_of(to * 16, 16), 16), :] = jnp.where(block < 2, upper, lower).astype(BF16)
            return inner

        lax.fori_loop(0, 8, collect, 0, unroll=2)
    send_all(gs, gl, g_send.at[0], g_recv.at[0], 16)

    up.wait()
    down.wait()
    lane = lax.broadcasted_iota(jnp.int32, (ROWS, N), 1)
    line = lax.broadcasted_iota(jnp.int32, (ROWS, N), 0)
    last_col = lane == N - 1
    last_line = line == ROWS - 1
    across, downs = [], []
    for p in range(2):
        cur = f[p]
        across.append(jnp.where(last_col, 0.0, pltpu.roll(cur, N - 1, 1) - cur))
        below = jnp.where(last_line, halo_r[1, p:p + 1, :], pltpu.roll(cur, ROWS - 1, 0))
        downs.append(jnp.where(last_line & (row == DEVS - 1), 0.0, below - cur))
    scale = w[...] / jnp.sqrt(across[0] * across[0] + across[1] * across[1]
                              + downs[0] * downs[0] + downs[1] * downs[1] + TV_EPS)
    above = halo_r[0]
    top_across = jnp.where(lax.broadcasted_iota(jnp.int32, (8, N), 1) == N - 1, 0.0, pltpu.roll(above, N - 1, 1) - above)
    top_down = [f[p, 0:1, :] - above[p:p + 1] for p in range(2)]
    top_scale = above[2:3] / jnp.sqrt(top_across[0:1] * top_across[0:1] + top_across[1:2] * top_across[1:2]
                                      + top_down[0] * top_down[0] + top_down[1] * top_down[1] + TV_EPS)
    for p in range(2):
        fa = scale * across[p]
        fd = scale * downs[p]
        top = jnp.where(row == 0, 0.0, top_scale * top_down[p])
        left = jnp.where(lane == 0, 0.0, pltpu.roll(fa, 1, 1))
        over = jnp.where(line == 0, top, pltpu.roll(fd, 1, 0))
        tvg[p] = TV_GAIN * ((left - fa) + (over - fd))

    xtab_in.wait()
    for g in range(GROUPS):

        for j in range(8):
            wait_bytes(r.at[g, pl.ds(0, 128)], b_recv.at[g, j])

        def gather(j, carry):
            lanes = pl.ds(pl.multiple_of(j * 128, 128), 128)
            for p in range(2):
                got = swap_blocks([
                    r[g, pl.ds(pl.multiple_of((4 * j + i) * 32, 32), 32), p * 128:(p + 1) * 128]
                    for i in range(4)])
                for c in range(4):
                    short = got[c]
                    other = pl.ds(pl.multiple_of(N + j * 128, 128), 128)
                    line = slice(c * 32, (c + 1) * 32)
                    cross = slice(128 + c * 32, 128 + (c + 1) * 32)
                    if p == 0:
                        lmat[line, lanes] = short
                        lmat[cross, other] = short
                    else:
                        lmat[line, other] = -short
                        lmat[cross, lanes] = short
            return carry

        lax.fori_loop(0, 8, gather, 0, unroll=8)

        if g == GROUPS - 1:
            wait_all(gl, g_recv.at[0])

            def unpack(j, carry):
                lanes = pl.ds(pl.multiple_of(j * 128, 128), 128)
                got = swap_blocks([gl[pl.ds(pl.multiple_of((4 * j + i) * 16, 16), 16), :] for i in range(4)])
                for hp in range(4):
                    acc[hp % 2, hp // 2 * 16:hp // 2 * 16 + 16, lanes] += got[hp].astype(F32)
                return carry

            lax.fori_loop(0, 8, unpack, 0, unroll=8)

        def inverse_x(xt, carry):
            cols = pl.ds(pl.multiple_of(xt * 256, 256), 256)
            both = dot(lmat[...], xtab[:, cols])
            real, imag = both[:128], both[128:]
            gr = jnp.zeros((32, 256), F32)
            gi = jnp.zeros((32, 256), F32)
            for c in range(PER):
                sr = s[0, g * PER + c, :, cols].astype(F32)
                si = s[1, g * PER + c, :, cols].astype(F32)
                br = real[c * 32:(c + 1) * 32]
                bi = imag[c * 32:(c + 1) * 32]
                gr += sr * br + si * bi
                gi += sr * bi - si * br
            if g == 0:
                acc[0, :, cols] = gr
                acc[1, :, cols] = gi
            else:
                part_s[xt, 0] = (acc[0, :, cols] + gr).astype(BF16)
                part_s[xt, 1] = (acc[1, :, cols] + gi).astype(BF16)
                pltpu.make_async_remote_copy(
                    part_s.at[xt], part_r.at[xt], p_send.at[xt], p_recv.at[xt],
                    device_id={"coil": 1 - coil}, device_id_type=pl.DeviceIdType.MESH).start()
            return carry

        lax.fori_loop(0, 4, inverse_x, 0)

    def finish(xt, carry):
        wait_bytes(part_r.at[xt], p_recv.at[xt])
        cols = pl.ds(pl.multiple_of(xt * 256, 256), 256)
        for p in range(2):
            comb[frame, xt, p] = part_s[xt, p].astype(F32) + part_r[xt, p].astype(F32) + tvg[p, :, cols]
        pltpu.make_async_remote_copy(
            comb.at[frame, xt], comb.at[frame, xt], c_send.at[xt], c_recv.at[xt],
            device_id={"frame": 1 - frame}, device_id_type=pl.DeviceIdType.MESH).start()
        pltpu.make_async_copy(comb.at[frame, xt], out_hbm.at[frame, xt], o_sem.at[0, xt]).start()
        return carry

    lax.fori_loop(0, 4, finish, 0)
    for xt in range(4):
        wait_bytes(comb.at[1 - frame, xt], c_recv.at[xt])
        pltpu.make_async_copy(comb.at[1 - frame, xt], out_hbm.at[1 - frame, xt], o_sem.at[1, xt]).start()
    for xt in range(4):
        wait_bytes(comb.at[frame, xt], c_send.at[xt])
        wait_bytes(part_s.at[xt], p_send.at[xt])
    wait_all(x, s_send.at[0])
    wait_all(fs, f_send.at[0])
    wait_all(gs, g_send.at[0])
    share.wait_send()
    for k in range(2):
        for xt in range(4):
            wait_bytes(comb.at[frame, xt], o_sem.at[k, xt])
    for g in range(GROUPS):
        wait_all(b.at[g], b_send.at[g])


def spread_column(values, which, column):
    line = jnp.where(which == 0, values[0:1], values[1:2])
    here = lax.broadcasted_iota(jnp.int32, (RANK, RANK), 0) == lax.broadcasted_iota(jnp.int32, (RANK, RANK), 1)
    column[...] = dot(jnp.where(here, line, 0.0).astype(BF16), jnp.ones((RANK, column.shape[1]), BF16))


def outer_kernel(v_hbm, g_hbm, out_hbm, v_ref, g_ref, first, second, out, in_sem, sem):
    g_in = [pltpu.make_async_copy(g_hbm.at[:, :, p], g_ref.at[:, :, p], in_sem.at[p]) for p in range(2)]
    v_in = pltpu.make_async_copy(v_hbm, v_ref, in_sem.at[2])
    v_in.start()
    for copy in g_in:
        copy.start()
    v_in.wait()
    values = v_ref[...].astype(F32)
    spread_column(values, 0, first)
    spread_column(values, 1, second)
    step = 4
    for p in range(2):
        g_in[p].wait()

        def some(block, carry):
            for top in range(0, ROWS, 8):
                for half in range(0, N, 256):
                    part = (slice(top, top + 8), slice(half, half + 256))
                    g0 = g_ref[0, half // 256, p, part[0], :]
                    g1 = g_ref[1, half // 256, p, part[0], :]
                    for k in range(step):
                        at = block * step + k
                        out[p, at, part[0], part[1]] = first[pl.ds(at, 1), :] * g0 + second[pl.ds(at, 1), :] * g1
            ranks = pl.ds(block * step, step)
            pltpu.make_async_copy(out.at[p, ranks], out_hbm.at[p, ranks], sem).start()
            return carry

        lax.fori_loop(0, RANK // step, some, 0)
    pltpu.make_async_copy(out, out_hbm, sem).wait()


def shards(factor_u, temporal_v, sensitivity, kspace_data, sample_mask, tv_weight):
    anywhere = pl.BlockSpec(memory_space=pltpu.HBM)
    dma = pltpu.SemaphoreType.DMA
    combined = pl.pallas_call(
        main_kernel,
        out_shape=jax.ShapeDtypeStruct((2, 4, 2, ROWS, 256), F32),
        in_specs=[anywhere] * 8,
        out_specs=anywhere,
        scratch_shapes=[
            pltpu.VMEM((2, RANK, ROWS, N), BF16),
            pltpu.VMEM((2, COILS, ROWS, N), BF16),
            pltpu.VMEM((2, 1, COILS, ROWS, N), BF16),
            pltpu.VMEM((ROWS, N), F32),
            pltpu.VMEM((2 * N, N), BF16),
            pltpu.VMEM((2, 4, 256, 512), BF16),
            pltpu.VMEM((1, N), jnp.int32),
            pltpu.VMEM((2, RANK), BF16),
            pltpu.VMEM((RANK, 512), F32),
            pltpu.VMEM((2, ROWS, N), F32),
            pltpu.VMEM((N // 2, 128), BF16),
            pltpu.VMEM((N // 2, 128), BF16),
            pltpu.VMEM((N // 2, 512), F32),
            pltpu.VMEM((N, 128), F32),
            pltpu.VMEM((4, 256, 128), F32),
            pltpu.VMEM((N, 256), BF16),
            pltpu.VMEM((GROUPS, N, 256), BF16),
            pltpu.VMEM((4, 512, 256), BF16),
            pltpu.VMEM((4, 512, 256), BF16),
            pltpu.VMEM((4, 256, 256), F32),
            pltpu.VMEM((GROUPS, N, 256), BF16),
            pltpu.VMEM((GROUPS, N, 256), BF16),
            pltpu.VMEM((N, 256), F32),
            pltpu.VMEM((N // 2, 128), BF16),
            pltpu.VMEM((N // 2, 128), BF16),
            pltpu.VMEM((256, 2 * N), BF16),
            pltpu.VMEM((2, ROWS, N), F32),
            pltpu.VMEM((2, 8, N), F32),
            pltpu.VMEM((2, 8, N), F32),
            pltpu.VMEM((4, 2, ROWS, 256), BF16),
            pltpu.VMEM((4, 2, ROWS, 256), BF16),
            pltpu.VMEM((2, 4, 2, ROWS, 256), F32),
            pltpu.VMEM((2, ROWS, N), F32),
            dma((4,)), dma((7,)), dma((2,)), dma((2,)),
            dma((1,)), dma((1,)), dma((1,)), dma((1,)), dma((1,)), dma((1,)), dma((GROUPS,)), dma((GROUPS, 8)),
            dma((1,)), dma((1,)), dma((4,)), dma((4,)), dma((4,)), dma((4,)), dma((2, 4)),
        ],
        compiler_params=pltpu.CompilerParams(
            collective_id=0, has_side_effects=True, vmem_limit_bytes=VMEM_LIMIT
        ),
        cost_estimate=pl.CostEstimate(flops=6 * 10**9, bytes_accessed=14 * 10**6, transcendentals=40000),
        name="frame_gradient",
    )(temporal_v, sample_mask, factor_u, sensitivity, kspace_data, tv_weight, jnp.asarray(x_table()), jnp.asarray(y_tables()))
    return pl.pallas_call(
        outer_kernel,
        out_shape=jax.ShapeDtypeStruct((2, RANK, ROWS, N), F32),
        in_specs=[anywhere] * 2,
        out_specs=anywhere,
        scratch_shapes=[
            pltpu.VMEM((2, RANK), BF16), pltpu.VMEM((2, 4, 2, ROWS, 256), F32),
            pltpu.VMEM((RANK, 256), F32), pltpu.VMEM((RANK, 256), F32),
            pltpu.VMEM((2, RANK, ROWS, N), F32), dma((3,)), dma,
        ],
        compiler_params=pltpu.CompilerParams(vmem_limit_bytes=VMEM_LIMIT),
        cost_estimate=pl.CostEstimate(flops=10**7, bytes_accessed=13 * 10**6, transcendentals=0),
        name="spread_over_rank",
    )(temporal_v, combined)


def solution(mesh):
    return jax.shard_map(
        shards,
        mesh=mesh,
        in_specs=(
            P(None, None, "row", None),
            P(),
            P(None, "coil", "row", None),
            P(None, "frame", "coil", "row", None),
            P("frame", None),
            P("row", None),
        ),
        out_specs=P(None, None, "row", None),
        check_vma=False,
    )
```

```python
import math

import jax
import jax.numpy as jnp
import numpy as np
from jax import lax
from jax.experimental import pallas as pl
from jax.experimental.pallas import tpu as pltpu
from jax.sharding import PartitionSpec as P

N = 1024
ROWS = 32
RANK = 48
COILS = 8
GROUPS = 2
PER = COILS // GROUPS
DEVS = 32
VMEM_LIMIT = 64 * 1024 * 1024 - 640 * 1024
TV_EPS = 0.25
TV_GAIN = 0.5
F32 = jnp.float32
BF16 = jnp.bfloat16


def angle_pair(product):
    angle = 2.0 * math.pi * (product % N) / N
    return np.cos(angle) / math.sqrt(N), np.sin(angle) / math.sqrt(N)


def x_table():
    at = np.arange(N)
    return np.concatenate(angle_pair(at[:, None] * at[None, :])).astype(jnp.bfloat16)


def y_tables():
    quarter = np.arange(N // 4)
    sides = []
    for q in range(4):
        cosine, sine = angle_pair((4 * quarter[:, None] + q) * quarter[None, :])
        sides.append((np.concatenate([cosine, sine], axis=1), np.concatenate([cosine.T, sine.T], axis=1)))
    return np.stack([np.stack([side[k] for side in sides]) for k in range(2)]).astype(jnp.bfloat16)


def swap_blocks(parts):
    lane = lax.broadcasted_iota(jnp.int32, parts[0].shape, 1)
    even = (lane // 32) % 2 == 0
    low = lane < 64
    a = list(parts)
    for x, y in ((0, 1), (2, 3)):
        first = jnp.where(even, a[x], pltpu.roll(a[y], 32, 1))
        second = jnp.where(even, pltpu.roll(a[x], 96, 1), a[y])
        a[x], a[y] = first, second
    for x, y in ((0, 2), (1, 3)):
        first = jnp.where(low, a[x], pltpu.roll(a[y], 64, 1))
        second = jnp.where(low, pltpu.roll(a[x], 64, 1), a[y])
        a[x], a[y] = first, second
    return a


def dot(a, b):
    return jnp.dot(a, b, preferred_element_type=F32)


def main_kernel(
    v_hbm, mask_hbm, u_hbm, s_hbm, d_hbm, w_hbm, xtab_hbm, ytab_hbm, out_hbm,
    u, s, d, w, xtab, ytab, mask_ref, v_ref, vcol, f, fs, fl, fy, dturn, mcol, x, land, uq, mis, bq, b, r,
    gacc, gs, gl, lmat, acc, halo_s, halo_r, part_s, part_r, comb, tvg,
    u_sem, in_sem, halo_send, halo_recv, s_send, s_recv, e_send, e_recv, f_send, f_recv, b_send, b_recv,
    g_send, g_recv, p_send, p_recv, c_send, c_recv, o_sem,
):
    row = lax.axis_index("row")
    frame = lax.axis_index("frame")
    coil = lax.axis_index("coil")

    names = ((v_hbm, v_ref), (s_hbm, s), (mask_hbm, mask_ref), (d_hbm, d), (ytab_hbm, ytab), (w_hbm, w), (xtab_hbm, xtab))
    in_copies = [pltpu.make_async_copy(src, dst, in_sem.at[q]) for q, (src, dst) in enumerate(names)]
    v_in, s_in, mask_in, d_in, ytab_in, w_in, xtab_in = in_copies
    u_copies = []
    for q in range(4):
        part = (q // 2, slice(None), pl.ds((q % 2) * 16, 16))
        u_copies.append(pltpu.make_async_copy(u_hbm.at[part], u.at[part], u_sem.at[q]))
    for copy in in_copies[:2] + u_copies + in_copies[2:]:
        copy.start()

    barrier = pltpu.get_barrier_semaphore()

    def greet(i, carry):
        @pl.when(i != row)
        def _():
            pl.semaphore_signal(barrier, inc=1, device_id={"row": i}, device_id_type=pl.DeviceIdType.MESH)
        return carry

    lax.fori_loop(0, DEVS, greet, 0)
    pl.semaphore_signal(barrier, inc=1, device_id={"coil": 1 - coil}, device_id_type=pl.DeviceIdType.MESH)
    pl.semaphore_signal(barrier, inc=1, device_id={"frame": 1 - frame}, device_id_type=pl.DeviceIdType.MESH)

    def send_all(src, dst, send_sem, recv_sem, size):
        mine = pl.ds(pl.multiple_of(row * size, size), size)

        def send(k, carry):
            to = (row + 13 * k) % DEVS
            pltpu.make_async_remote_copy(
                src.at[pl.ds(pl.multiple_of(to * size, size), size)], dst.at[mine], send_sem, recv_sem,
                device_id={"row": to}, device_id_type=pl.DeviceIdType.MESH).start()
            return carry

        lax.fori_loop(1, DEVS, send, 0)
        dst[mine, :] = src[mine, :]

    def wait_bytes(ref, sem):
        pltpu.make_async_copy(ref, ref, sem).wait()

    def wait_all(ref, sem):
        wait_bytes(ref.at[pl.ds(0, ref.shape[0] // DEVS * (DEVS - 1))], sem)

    s_in.wait()

    def lay_maps(k, carry):
        j = k
        lanes = pl.ds(pl.multiple_of(j * 128, 128), 128)
        for p in range(2):
            w4 = swap_blocks([s[p, frame * PER + c, :, lanes] for c in range(4)])
            for i in range(4):
                x[pl.ds(pl.multiple_of((j * 4 + i) * 32, 32), 32), p * 128:(p + 1) * 128] = w4[i]
        return carry

    lax.fori_loop(0, 8, lay_maps, 0, unroll=8)
    pl.semaphore_wait(barrier, DEVS + 1)
    send_all(x, land.at[frame], s_send.at[0], s_recv.at[0], 32)

    v_in.wait()
    spread_column(v_ref[...].astype(F32), frame, vcol)
    for q in range(4):
        u_copies[q].wait()
        p, top = q // 2, (q % 2) * 16
        for half in range(2):
            total = jnp.zeros((16, 512), F32)
            for k in range(RANK):
                total += vcol[k:k + 1, :] * u[p, k, top:top + 16, half * 512:(half + 1) * 512].astype(F32)
            f[p, top:top + 16, half * 512:(half + 1) * 512] = total

    def send_frame(k, carry):
        j = k
        lanes = pl.ds(pl.multiple_of(j * 128, 128), 128)
        w4 = swap_blocks([f[hp % 2, hp // 2 * 16:hp // 2 * 16 + 16, lanes] for hp in range(4)])
        for i in range(4):
            to = j * 4 + i
            fs[pl.ds(pl.multiple_of(to * 16, 16), 16), :] = w4[i].astype(BF16)
        return carry

    lax.fori_loop(0, 8, send_frame, 0, unroll=4)
    send_all(fs, fl, f_send.at[0], f_recv.at[0], 16)

    w_in.wait()
    halo_s[...] = jnp.zeros_like(halo_s)
    for p in range(2):
        halo_s[0, p:p + 1, :] = f[p, 0:1, :]
        halo_s[1, p:p + 1, :] = f[p, 31:32, :]
    halo_s[1, 2:3, :] = w[31:32, :]
    up = pltpu.make_async_remote_copy(
        halo_s.at[0], halo_r.at[1], halo_send.at[0], halo_recv.at[1],
        device_id={"row": (row + DEVS - 1) % DEVS}, device_id_type=pl.DeviceIdType.MESH)
    down = pltpu.make_async_remote_copy(
        halo_s.at[1], halo_r.at[0], halo_send.at[1], halo_recv.at[0],
        device_id={"row": (row + 1) % DEVS}, device_id_type=pl.DeviceIdType.MESH)
    up.start()
    down.start()

    d_in.wait()
    mask_in.wait()
    ytab_in.wait()

    def fold_back(at):
        part = [bq[q, at, :] for q in range(4)]
        plus, minus = part[0] + part[2], part[0] - part[2]
        other, cross = part[1] + part[3], part[1] - part[3]
        turned = jnp.concatenate([-cross[:, 128:], cross[:, :128]], axis=1)
        return plus + other, minus + turned, plus - other, minus - turned

    def measured(g, carry):
        keep = -mask_ref[...].astype(F32)
        for p in range(2):
            dturn[...] = (d[p, 0, pl.ds(g * PER, PER)].reshape(128, N).astype(F32) * keep).T
            for q in range(4):
                value = dturn[pl.ds(q, 256, stride=4), :].astype(BF16)
                if p == 0:
                    mis[q, :256, :128] = value
                    mis[q, 256:, 128:] = value
                else:
                    mis[q, :256, 128:] = value
                    mis[q, 256:, :128] = -value
        for q in range(4):
            bq[q] = dot(ytab[1, q], mis[q])

        def back(k, inner):
            turn = k
            for p, value in enumerate(fold_back(pl.ds(pl.multiple_of(turn * 32, 32), 32))):
                b[g, pl.ds(pl.multiple_of(p * 256 + turn * 32, 32), 32), :] = value.astype(BF16)
            return inner

        lax.fori_loop(0, 8, back, 0, unroll=2)
        return carry

    def send_measured(g):
        mine = pl.ds(pl.multiple_of(row * 32, 32), 32)
        own = pltpu.make_async_copy(b.at[g, mine], r.at[g, mine], b_recv.at[g, row // 4])

        def send(k, carry):
            to = (row + 13 * k) % DEVS
            pltpu.make_async_remote_copy(
                b.at[g, pl.ds(pl.multiple_of(to * 32, 32), 32)], r.at[g, mine], b_send.at[g], b_recv.at[g, row // 4],
                device_id={"row": to}, device_id_type=pl.DeviceIdType.MESH).start()
            return carry

        lax.fori_loop(1, DEVS, send, 0)
        own.start()

    lax.fori_loop(0, GROUPS, measured, 0)
    send_measured(0)

    dturn[...] = jnp.broadcast_to(mask_ref[...].astype(F32), (128, N)).T
    for q in range(4):
        mcol[q] = dturn[pl.ds(q, 256, stride=4), :]
    wait_all(land.at[frame], s_recv.at[0])
    share = pltpu.make_async_remote_copy(
        land.at[frame], land.at[frame], e_send.at[0], e_recv.at[0],
        device_id={"frame": 1 - frame}, device_id_type=pl.DeviceIdType.MESH)
    share.start()
    wait_all(fl, f_recv.at[0])
    send_measured(1)
    source = lax.broadcasted_iota(jnp.int32, (128, 512), 0)
    target = lax.broadcasted_iota(jnp.int32, (128, 512), 1)
    same = (source // 32 == target // 128) & (source % 32 == target % 32)
    copies = jnp.where(same, 1.0, 0.0).astype(BF16)
    fy[...] = dot(fl[...], copies)

    for turn_g in range(2):
        g = (frame + turn_g) % 2
        if turn_g == 1:
            wait_bytes(land.at[1 - frame], e_recv.at[0])

        def spread(k, inner):
            part = []
            for p in range(4):
                at = p * 8 + k
                maps = land[g, pl.ds(pl.multiple_of(at * 32, 32), 32), :].astype(F32)
                image = fy[pl.ds(pl.multiple_of(at * 16, 16), 16), :]
                fr = jnp.concatenate([image[:, :128], image[:, 256:384]], axis=0)
                fi = jnp.concatenate([image[:, 128:256], image[:, 384:]], axis=0)
                sr, si = maps[:, :128], maps[:, 128:]
                part.append((sr * fr - si * fi, sr * fi + si * fr))
            plus = [part[0][z] + part[2][z] for z in range(2)]
            minus = [part[0][z] - part[2][z] for z in range(2)]
            other = [part[1][z] + part[3][z] for z in range(2)]
            cross = [part[1][z] - part[3][z] for z in range(2)]
            values = (
                (plus[0] + other[0], plus[1] + other[1]),
                (minus[0] + cross[1], minus[1] - cross[0]),
                (plus[0] - other[0], plus[1] - other[1]),
                (minus[0] - cross[1], minus[1] + cross[0]),
            )
            at = pl.multiple_of(k * 32, 32)
            for q, (real, imag) in enumerate(values):
                real, imag = real.astype(BF16), imag.astype(BF16)
                uq[q, pl.ds(at, 32), :128] = real
                uq[q, pl.ds(at, 32), 128:] = imag
                uq[q, pl.ds(256 + at, 32), :128] = imag
                uq[q, pl.ds(256 + at, 32), 128:] = -real
            return inner

        lax.fori_loop(0, 8, spread, 0, unroll=2)
        for q in range(4):
            spectrum = dot(ytab[0, q], uq[q])
            keep = mcol[q]
            real = (keep * spectrum[:, :128]).astype(BF16)
            imag = (keep * spectrum[:, 128:]).astype(BF16)
            mis[q, :256, :128] = real
            mis[q, :256, 128:] = imag
            mis[q, 256:, :128] = -imag
            mis[q, 256:, 128:] = real
        for q in range(4):
            bq[q] = dot(ytab[1, q], mis[q])

        def collect(k, inner):
            turn = k
            for p, value in enumerate(fold_back(pl.ds(pl.multiple_of(turn * 32, 32), 32))):
                to = p * 8 + turn
                rows = pl.ds(pl.multiple_of(to * 32, 32), 32)
                maps = land[g, rows, :].astype(F32)
                sr, si = maps[:, :128], maps[:, 128:]
                ar, ai = value[:, :128], value[:, 128:]
                gr = sr * ar + si * ai
                gi = sr * ai - si * ar

                if turn_g == 0:
                    gacc[rows, :128] = gr
                    gacc[rows, 128:] = gi
                else:
                    whole = []
                    for z in (gacc[rows, :128] + gr, gacc[rows, 128:] + gi):
                        z = z + pltpu.roll(z, 64, 1)
                        whole.append(z + pltpu.roll(z, 32, 1))
                    block = lax.broadcasted_iota(jnp.int32, (16, 128), 1) // 32
                    upper = jnp.where(block == 0, whole[0][:16], whole[1][:16])
                    lower = jnp.where(block == 2, whole[0][16:], whole[1][16:])
                    gs[pl.ds(pl.multiple_of(to * 16, 16), 16), :] = jnp.where(block < 2, upper, lower).astype(BF16)
            return inner

        for part in range(2):
            lax.fori_loop(4 * part, 4 * part + 4, collect, 0, unroll=2)
            if turn_g == 1:
                def send_image(k, inner):
                    to = (k + row // 8) % 4 * 8 + 4 * part + k // 4
                    mine = pl.ds(pl.multiple_of(row * 16, 16), 16)

                    @pl.when(to != row)
                    def _():
                        pltpu.make_async_remote_copy(
                            gs.at[pl.ds(pl.multiple_of(to * 16, 16), 16)], gl.at[mine], g_send.at[0], g_recv.at[0],
                            device_id={"row": to}, device_id_type=pl.DeviceIdType.MESH).start()
                    return inner

                lax.fori_loop(0, 16, send_image, 0)
    own_rows = pl.ds(pl.multiple_of(row * 16, 16), 16)
    gl[own_rows, :] = gs[own_rows, :]

    up.wait()
    down.wait()
    lane = lax.broadcasted_iota(jnp.int32, (ROWS, N), 1)
    line = lax.broadcasted_iota(jnp.int32, (ROWS, N), 0)
    last_col = lane == N - 1
    last_line = line == ROWS - 1
    across, downs = [], []
    for p in range(2):
        cur = f[p]
        across.append(jnp.where(last_col, 0.0, pltpu.roll(cur, N - 1, 1) - cur))
        below = jnp.where(last_line, halo_r[1, p:p + 1, :], pltpu.roll(cur, ROWS - 1, 0))
        downs.append(jnp.where(last_line & (row == DEVS - 1), 0.0, below - cur))
    scale = w[...] / jnp.sqrt(across[0] * across[0] + across[1] * across[1]
                              + downs[0] * downs[0] + downs[1] * downs[1] + TV_EPS)
    above = halo_r[0]
    top_across = jnp.where(lax.broadcasted_iota(jnp.int32, (8, N), 1) == N - 1, 0.0, pltpu.roll(above, N - 1, 1) - above)
    top_down = [f[p, 0:1, :] - above[p:p + 1] for p in range(2)]
    top_scale = above[2:3] / jnp.sqrt(top_across[0:1] * top_across[0:1] + top_across[1:2] * top_across[1:2]
                                      + top_down[0] * top_down[0] + top_down[1] * top_down[1] + TV_EPS)
    for p in range(2):
        fa = scale * across[p]
        fd = scale * downs[p]
        top = jnp.where(row == 0, 0.0, top_scale * top_down[p])
        left = jnp.where(lane == 0, 0.0, pltpu.roll(fa, 1, 1))
        over = jnp.where(line == 0, top, pltpu.roll(fd, 1, 0))
        tvg[p] = TV_GAIN * ((left - fa) + (over - fd))

    xtab_in.wait()
    for g in range(GROUPS):

        for j in range(8):
            wait_bytes(r.at[g, pl.ds(0, 128)], b_recv.at[g, j])

        def gather(j, carry):
            lanes = pl.ds(pl.multiple_of(j * 128, 128), 128)
            for p in range(2):
                got = swap_blocks([
                    r[g, pl.ds(pl.multiple_of((4 * j + i) * 32, 32), 32), p * 128:(p + 1) * 128]
                    for i in range(4)])
                for c in range(4):
                    short = got[c]
                    other = pl.ds(pl.multiple_of(N + j * 128, 128), 128)
                    line = slice(c * 32, (c + 1) * 32)
                    cross = slice(128 + c * 32, 128 + (c + 1) * 32)
                    if p == 0:
                        lmat[line, lanes] = short
                        lmat[cross, other] = short
                    else:
                        lmat[line, other] = -short
                        lmat[cross, lanes] = short
            return carry

        lax.fori_loop(0, 8, gather, 0, unroll=8)

        if g == GROUPS - 1:
            wait_all(gl, g_recv.at[0])

            def unpack(j, carry):
                lanes = pl.ds(pl.multiple_of(j * 128, 128), 128)
                got = swap_blocks([gl[pl.ds(pl.multiple_of((4 * j + i) * 16, 16), 16), :] for i in range(4)])
                for hp in range(4):
                    acc[hp % 2, hp // 2 * 16:hp // 2 * 16 + 16, lanes] += got[hp].astype(F32)
                return carry

            lax.fori_loop(0, 8, unpack, 0, unroll=8)

        def inverse_x(xt, carry):
            cols = pl.ds(pl.multiple_of(xt * 256, 256), 256)
            both = dot(lmat[...], xtab[:, cols])
            real, imag = both[:128], both[128:]
            gr = jnp.zeros((32, 256), F32)
            gi = jnp.zeros((32, 256), F32)
            for c in range(PER):
                sr = s[0, g * PER + c, :, cols].astype(F32)
                si = s[1, g * PER + c, :, cols].astype(F32)
                br = real[c * 32:(c + 1) * 32]
                bi = imag[c * 32:(c + 1) * 32]
                gr += sr * br + si * bi
                gi += sr * bi - si * br
            if g == 0:
                acc[0, :, cols] = gr
                acc[1, :, cols] = gi
            else:
                part_s[xt, 0] = (acc[0, :, cols] + gr).astype(BF16)
                part_s[xt, 1] = (acc[1, :, cols] + gi).astype(BF16)
                pltpu.make_async_remote_copy(
                    part_s.at[xt], part_r.at[xt], p_send.at[xt], p_recv.at[xt],
                    device_id={"coil": 1 - coil}, device_id_type=pl.DeviceIdType.MESH).start()
            return carry

        lax.fori_loop(0, 4, inverse_x, 0)

    def finish(xt, carry):
        wait_bytes(part_r.at[xt], p_recv.at[xt])
        cols = pl.ds(pl.multiple_of(xt * 256, 256), 256)
        for p in range(2):
            comb[frame, xt, p] = part_s[xt, p].astype(F32) + part_r[xt, p].astype(F32) + tvg[p, :, cols]
        pltpu.make_async_remote_copy(
            comb.at[frame, xt], comb.at[frame, xt], c_send.at[xt], c_recv.at[xt],
            device_id={"frame": 1 - frame}, device_id_type=pl.DeviceIdType.MESH).start()
        pltpu.make_async_copy(comb.at[frame, xt], out_hbm.at[frame, xt], o_sem.at[0, xt]).start()
        return carry

    lax.fori_loop(0, 4, finish, 0)
    for xt in range(4):
        wait_bytes(comb.at[1 - frame, xt], c_recv.at[xt])
        pltpu.make_async_copy(comb.at[1 - frame, xt], out_hbm.at[1 - frame, xt], o_sem.at[1, xt]).start()
    for xt in range(4):
        wait_bytes(comb.at[frame, xt], c_send.at[xt])
        wait_bytes(part_s.at[xt], p_send.at[xt])
    wait_all(x, s_send.at[0])
    wait_all(fs, f_send.at[0])
    wait_all(gs, g_send.at[0])
    share.wait_send()
    for k in range(2):
        for xt in range(4):
            wait_bytes(comb.at[frame, xt], o_sem.at[k, xt])
    for g in range(GROUPS):
        wait_all(b.at[g], b_send.at[g])


def spread_column(values, which, column):
    line = jnp.where(which == 0, values[0:1], values[1:2])
    here = lax.broadcasted_iota(jnp.int32, (RANK, RANK), 0) == lax.broadcasted_iota(jnp.int32, (RANK, RANK), 1)
    column[...] = dot(jnp.where(here, line, 0.0).astype(BF16), jnp.ones((RANK, column.shape[1]), BF16))


def outer_kernel(v_hbm, g_hbm, out_hbm, v_ref, g_ref, first, second, out, in_sem, sem):
    g_in = [pltpu.make_async_copy(g_hbm.at[:, :, p], g_ref.at[:, :, p], in_sem.at[p]) for p in range(2)]
    v_in = pltpu.make_async_copy(v_hbm, v_ref, in_sem.at[2])
    v_in.start()
    for copy in g_in:
        copy.start()
    v_in.wait()
    values = v_ref[...].astype(F32)
    spread_column(values, 0, first)
    spread_column(values, 1, second)
    step = 2
    for p in range(2):
        g_in[p].wait()

        def some(block, carry):
            for top in range(0, ROWS, 8):
                for half in range(0, N, 256):
                    part = (slice(top, top + 8), slice(half, half + 256))
                    g0 = g_ref[0, half // 256, p, part[0], :]
                    g1 = g_ref[1, half // 256, p, part[0], :]
                    for k in range(step):
                        at = block * step + k
                        out[p, at, part[0], part[1]] = first[pl.ds(at, 1), :] * g0 + second[pl.ds(at, 1), :] * g1
            ranks = pl.ds(block * step, step)
            pltpu.make_async_copy(out.at[p, ranks], out_hbm.at[p, ranks], sem).start()
            return carry

        lax.fori_loop(0, RANK // step, some, 0)
    pltpu.make_async_copy(out, out_hbm, sem).wait()


def shards(factor_u, temporal_v, sensitivity, kspace_data, sample_mask, tv_weight):
    anywhere = pl.BlockSpec(memory_space=pltpu.HBM)
    dma = pltpu.SemaphoreType.DMA
    combined = pl.pallas_call(
        main_kernel,
        out_shape=jax.ShapeDtypeStruct((2, 4, 2, ROWS, 256), F32),
        in_specs=[anywhere] * 8,
        out_specs=anywhere,
        scratch_shapes=[
            pltpu.VMEM((2, RANK, ROWS, N), BF16),
            pltpu.VMEM((2, COILS, ROWS, N), BF16),
            pltpu.VMEM((2, 1, COILS, ROWS, N), BF16),
            pltpu.VMEM((ROWS, N), F32),
            pltpu.VMEM((2 * N, N), BF16),
            pltpu.VMEM((2, 4, 256, 512), BF16),
            pltpu.VMEM((1, N), jnp.int32),
            pltpu.VMEM((2, RANK), BF16),
            pltpu.VMEM((RANK, 512), F32),
            pltpu.VMEM((2, ROWS, N), F32),
            pltpu.VMEM((N // 2, 128), BF16),
            pltpu.VMEM((N // 2, 128), BF16),
            pltpu.VMEM((N // 2, 512), F32),
            pltpu.VMEM((N, 128), F32),
            pltpu.VMEM((4, 256, 128), F32),
            pltpu.VMEM((N, 256), BF16),
            pltpu.VMEM((GROUPS, N, 256), BF16),
            pltpu.VMEM((4, 512, 256), BF16),
            pltpu.VMEM((4, 512, 256), BF16),
            pltpu.VMEM((4, 256, 256), F32),
            pltpu.VMEM((GROUPS, N, 256), BF16),
            pltpu.VMEM((GROUPS, N, 256), BF16),
            pltpu.VMEM((N, 256), F32),
            pltpu.VMEM((N // 2, 128), BF16),
            pltpu.VMEM((N // 2, 128), BF16),
            pltpu.VMEM((256, 2 * N), BF16),
            pltpu.VMEM((2, ROWS, N), F32),
            pltpu.VMEM((2, 8, N), F32),
            pltpu.VMEM((2, 8, N), F32),
            pltpu.VMEM((4, 2, ROWS, 256), BF16),
            pltpu.VMEM((4, 2, ROWS, 256), BF16),
            pltpu.VMEM((2, 4, 2, ROWS, 256), F32),
            pltpu.VMEM((2, ROWS, N), F32),
            dma((4,)), dma((7,)), dma((2,)), dma((2,)),
            dma((1,)), dma((1,)), dma((1,)), dma((1,)), dma((1,)), dma((1,)), dma((GROUPS,)), dma((GROUPS, 8)),
            dma((1,)), dma((1,)), dma((4,)), dma((4,)), dma((4,)), dma((4,)), dma((2, 4)),
        ],
        compiler_params=pltpu.CompilerParams(
            collective_id=0, has_side_effects=True, vmem_limit_bytes=VMEM_LIMIT
        ),
        cost_estimate=pl.CostEstimate(flops=6 * 10**9, bytes_accessed=14 * 10**6, transcendentals=40000),
        name="frame_gradient",
    )(temporal_v, sample_mask, factor_u, sensitivity, kspace_data, tv_weight, jnp.asarray(x_table()), jnp.asarray(y_tables()))
    return pl.pallas_call(
        outer_kernel,
        out_shape=jax.ShapeDtypeStruct((2, RANK, ROWS, N), F32),
        in_specs=[anywhere] * 2,
        out_specs=anywhere,
        scratch_shapes=[
            pltpu.VMEM((2, RANK), BF16), pltpu.VMEM((2, 4, 2, ROWS, 256), F32),
            pltpu.VMEM((RANK, 256), F32), pltpu.VMEM((RANK, 256), F32),
            pltpu.VMEM((2, RANK, ROWS, N), F32), dma((3,)), dma,
        ],
        compiler_params=pltpu.CompilerParams(vmem_limit_bytes=VMEM_LIMIT),
        cost_estimate=pl.CostEstimate(flops=10**7, bytes_accessed=13 * 10**6, transcendentals=0),
        name="spread_over_rank",
    )(temporal_v, combined)


def solution(mesh):
    return jax.shard_map(
        shards,
        mesh=mesh,
        in_specs=(
            P(None, None, "row", None),
            P(),
            P(None, "coil", "row", None),
            P(None, "frame", "coil", "row", None),
            P("frame", None),
            P("row", None),
        ),
        out_specs=P(None, None, "row", None),
        check_vma=False,
    )
```
